512 devices in a mesh: row: 32 (over x_lo, z, core), col: 16 (over x_hi, y).
Axes of the slice: x: 4 (x_hi: 2, x_lo: 2; x = x_hi * 2 + x_lo), y: 8, z: 8, core: 2. Of those that a mesh axis runs over, the one named last changes fastest.
Arguments:
- features: bfloat16 [65536, 128], P(('row', 'col')), may hold values from -6 to 6
- degrees: int32 [65536], P(('row', 'col')), may hold values from 16 to 256
- proj_weight: bfloat16 [128, 512], replicated, may hold values from -0.5 to 0.5
- bias: float32 [512], replicated, may hold values from -3 to 3
- grad_out: bfloat16 [65536, 512], P(('row', 'col')), may hold values from -6 to 6
- tile_slots: int32 [32, 16, 32, 2], P('row', 'col'), may hold values from -1 to 31, as said below
- tile_values: bfloat16 [32, 16, 32, 128, 128], P('row', 'col'), may hold values from -4 to 4
Outputs:
- activations: bfloat16 [65536, 512], P(('row', 'col'))
- grad_weight: float32 [128, 512], replicated
- grad_bias: float32 [512], replicated
- grad_features: bfloat16 [65536, 128], P(('row', 'col'))
The draws below stay inside these ranges and needn't reach their ends.
Inputs may be any that keep to these rules, and one draw needn't show every extreme that they name: `tile_slots`: entry [r, c, k] gives slot k's tile row (below 16) and tile column (below 32) in grid cell (r, c)'s block, both -1 for an empty slot. Live slots come first, hold distinct positions and stand in ascending order of tile column. Every grid cell has at least 4 live slots, and one grid cell has all 32 live.
All inputs are finite; a program needn't handle non-finite values.
Results may differ from the reference program's by a relative error of at most 0.0062.
Values may be sent and summed in bfloat16 or wider, within the bound.
A program may use at most 64 MiB of HBM per device.

```python
import jax
import jax.numpy as jnp
from jax import lax

F_IN = 128
HID = 512
NODE_DEV = 128
TILE = 128
NODES = 65536
ROW_TILES = 16
COL_TILES = 32
K_MAX = 32
N_ROW = 32
N_COL = 16


def draw_tile_slots(key, part):
    key = jax.random.fold_in(key, 11)
    key_counts = jax.random.fold_in(key, 1)
    key_busiest = jax.random.fold_in(key, 2)
    key_places = jax.random.fold_in(key, 3)
    cell_count = N_ROW * N_COL
    position_count = ROW_TILES * COL_TILES
    lowest = max(K_MAX // 8, 1)
    counts = jax.random.randint(key_counts, (cell_count,), lowest, K_MAX // 2 + 1)
    busiest = jax.random.randint(key_busiest, (), 0, cell_count)
    counts = jnp.where(jnp.arange(cell_count) == busiest, K_MAX, counts)
    cell_keys = jax.random.split(key_places, cell_count)
    shuffled = jax.vmap(lambda single: jax.random.permutation(single, position_count))(cell_keys)[:, :K_MAX]
    slot_index = jnp.arange(K_MAX)
    occupied = slot_index[None, :] < counts[:, None]
    picked = jnp.where(occupied, shuffled, position_count)
    ordered = jnp.sort(picked, axis=1)
    filled = ordered < position_count
    tile_rows = jnp.where(filled, ordered % ROW_TILES, -1)
    tile_cols = jnp.where(filled, ordered // ROW_TILES, -1)
    both = jnp.stack([tile_rows, tile_cols], axis=-1)
    return both.reshape(N_ROW, N_COL, K_MAX, 2).astype(jnp.int32)


def with_ends(array, rng, smallest, top_value):
    longest = array.shape.index(max(array.shape))
    spots = []
    for shift in (0, 1):
        where = [jax.random.randint(jax.random.fold_in(rng, axis), (), 0, length) for axis, length in enumerate(array.shape)]
        where[longest] = (where[longest] + shift) % array.shape[longest]
        spots.append(tuple(where))
    return array.at[spots[0]].set(smallest).at[spots[1]].set(top_value)


def levels(stream_key, dims, cuts, least, top_value):
    loudness = 1.0
    for axis_at, parts in cuts:
        heights = jax.random.uniform(jax.random.fold_in(jax.random.fold_in(stream_key, 6), axis_at), (parts,), jnp.float32, least / len(cuts), top_value / len(cuts))
        loudness = loudness * jnp.repeat(jnp.exp(heights), dims[axis_at] // parts).reshape((-1,) + (1,) * (len(dims) - 1 - axis_at))
    return loudness


def noise(stream_key, dims, deviation, limit, shards=(), held_as=jnp.bfloat16):
    gain = levels(stream_key, dims, shards, -0.22, 0.18) if shards else 1.0
    entries = jax.random.normal(stream_key, dims, jnp.float32) * deviation * gain
    return jnp.minimum(jnp.maximum(entries, -limit), limit).astype(held_as)


def setup_inputs(seed: int = 0) -> dict:
    keys = jax.random.split(jax.random.key(seed), 8)
    return {
        "features": noise(keys[0], (NODES, F_IN), 1.0, 6.0, ((0, 512),)),
        "degrees": with_ends(jax.random.randint(keys[1], (NODES,), 16, 257), jax.random.fold_in(keys[1], 1), 16, 256).astype(jnp.int32),
        "proj_weight": noise(keys[2], (F_IN, HID), F_IN ** -0.5, 0.5),
        "bias": noise(keys[3], (HID,), 0.5, 3.0, (), jnp.float32),
        "grad_out": noise(keys[4], (NODES, HID), 1.0, 6.0, ((0, 512),)),
        "tile_slots": draw_tile_slots(jax.random.fold_in(keys[7], 71), 0),
        "tile_values": noise(keys[6], (N_ROW, N_COL, K_MAX, TILE, TILE), 1.0, 4.0, ((0, 32), (1, 16))),
    }


def gelu_tanh(values):
    return jax.nn.gelu(values, approximate=True)

def block_product(values, slots, columns, row_tiles):
    tile_size = values.shape[1]
    width = columns.shape[1]
    stacked = columns.reshape(-1, tile_size, width)
    occupied = slots[:, 0] >= 0
    tile_rows = jnp.maximum(slots[:, 0], 0)
    tile_cols = jnp.maximum(slots[:, 1], 0)
    picked = stacked[tile_cols].astype(jnp.float32)
    products = jnp.einsum('kij,kjf->kif', values.astype(jnp.float32), picked)
    products = jnp.where(occupied[:, None, None], products, jnp.float32(0.0))
    totals = jnp.zeros((row_tiles, tile_size, width), jnp.float32).at[tile_rows].add(products)
    return totals.reshape(row_tiles * tile_size, width)

def block_product_t(values, slots, rows_in, col_tiles):
    tile_size = values.shape[1]
    width = rows_in.shape[1]
    stacked = rows_in.reshape(-1, tile_size, width)
    occupied = slots[:, 0] >= 0
    tile_rows = jnp.maximum(slots[:, 0], 0)
    tile_cols = jnp.maximum(slots[:, 1], 0)
    picked = stacked[tile_rows].astype(jnp.float32)
    products = jnp.einsum('kij,kif->kjf', values.astype(jnp.float32), picked)
    products = jnp.where(occupied[:, None, None], products, jnp.float32(0.0))
    totals = jnp.zeros((col_tiles, tile_size, width), jnp.float32).at[tile_cols].add(products)
    return totals.reshape(col_tiles * tile_size, width)

def reference(features, degrees, proj_weight, bias, grad_out, tile_slots, tile_values):
    norm = lax.rsqrt(degrees.astype(jnp.float32))
    scaled_in = (features.astype(jnp.float32) * norm[:, None]).astype(jnp.bfloat16)
    scaled_grid = scaled_in.reshape(N_ROW, N_COL, NODE_DEV, F_IN)

    def row_block(grid_row):

        def add_cell(carry, grid_col):
            cols_in = jnp.take(scaled_grid, grid_col, axis=1).reshape(N_ROW * NODE_DEV, F_IN)
            term = block_product(tile_values[grid_row, grid_col], tile_slots[grid_row, grid_col], cols_in, ROW_TILES)
            return (carry + term, None)
        start = jnp.zeros((ROW_TILES * TILE, F_IN), jnp.float32)
        result, unused = lax.scan(add_cell, start, jnp.arange(N_COL, dtype=jnp.int32))
        return result
    smooth = lax.map(row_block, jnp.arange(N_ROW, dtype=jnp.int32)).reshape(NODES, F_IN)
    smoothed = (norm[:, None] * smooth).astype(jnp.bfloat16)
    pre = jnp.dot(smoothed, proj_weight, preferred_element_type=jnp.float32) + bias[None, :]
    activations, backward = jax.vjp(gelu_tanh, pre)
    dpre = backward(grad_out.astype(jnp.float32))[0]
    dpre_b = dpre.astype(jnp.bfloat16)
    factor = NODES ** (-0.5)
    grad_weight = lax.dot_general(smoothed, dpre_b, (((0,), (0,)), ((), ())), preferred_element_type=jnp.float32) * factor
    grad_bias = lax.optimization_barrier(jnp.sum(dpre, axis=0)) * factor
    projected = lax.dot_general(dpre_b, proj_weight, (((1,), (1,)), ((), ())), preferred_element_type=jnp.float32)
    back_in = (projected * norm[:, None]).astype(jnp.bfloat16)
    back_grid = back_in.reshape(N_ROW, N_COL * NODE_DEV, F_IN)

    def col_block(grid_col):

        def add_cell(carry, grid_row):
            rows_in = jnp.take(back_grid, grid_row, axis=0)
            term = block_product_t(tile_values[grid_row, grid_col], tile_slots[grid_row, grid_col], rows_in, COL_TILES)
            return (carry + term, None)
        start = jnp.zeros((COL_TILES * TILE, F_IN), jnp.float32)
        result, unused = lax.scan(add_cell, start, jnp.arange(N_ROW, dtype=jnp.int32))
        return result
    back_cols = lax.map(col_block, jnp.arange(N_COL, dtype=jnp.int32))
    back_sum = back_cols.reshape(N_COL, N_ROW, NODE_DEV, F_IN).transpose(1, 0, 2, 3).reshape(NODES, F_IN)
    grad_features = (norm[:, None] * back_sum).astype(jnp.bfloat16)
    return (activations.astype(jnp.bfloat16), grad_weight, grad_bias, grad_features)
```

```python
import jax
import jax.numpy as jnp
from jax import lax
from jax.experimental import pallas as pl
from jax.experimental.pallas import tpu as pltpu
from jax.sharding import PartitionSpec as P

MESH = pl.DeviceIdType.MESH
BF16 = jnp.bfloat16
F32 = jnp.float32

N = 128
HID = 512
K = 32
NZ = 8
FAR = (4, 3, 5, 2, 6, 1, 7)
NEAR = (1, 7, 2, 6, 3, 5, 4)
PERM, COLP, KEEPF, LASTR, HASR = 0, 32, 64, 96, 112
ROWK, KEEPB, LASTC, HASC = 128, 160, 192, 224


def index_table(slots):
    rows, cols = slots[:, 0], slots[:, 1]
    live = rows >= 0
    k = jnp.arange(K, dtype=jnp.int32)
    row_key = jnp.where(live, rows, 16)
    key = row_key * K + k
    rank = jnp.sum((key[None, :] < key[:, None]).astype(jnp.int32), axis=1)
    chosen = rank[None, :] == k[:, None]

    def pick(values):
        return jnp.sum(jnp.where(chosen, values[None, :], 0), axis=1)

    perm, colp, rowp = pick(k), pick(jnp.maximum(cols, 0)), pick(row_key)
    keepf = jnp.concatenate([jnp.zeros((1,), jnp.int32), (rowp[1:] == rowp[:-1]).astype(jnp.int32)])
    col_key = jnp.where(live, cols, 32)
    keepb = jnp.concatenate([jnp.zeros((1,), jnp.int32), (col_key[1:] == col_key[:-1]).astype(jnp.int32)])

    def ends(keys, count):
        places = jnp.arange(count, dtype=jnp.int32)[:, None]
        last = jnp.sum((keys[None, :] <= places).astype(jnp.int32), axis=1) - 1
        has = jnp.max((keys[None, :] == places).astype(jnp.int32), axis=1)
        return jnp.maximum(last, 0), has

    lastr, hasr = ends(row_key, 16)
    lastc, hasc = ends(col_key, 32)
    return jnp.concatenate([perm, colp, keepf, lastr, hasr, jnp.maximum(rows, 0), keepb, lastc, hasc])


def layer(tab, feat, deg, w, bias, gout, vals_hbm,
          act, gw, gb, gf,
          vals, xg, ps, xs2, xr2, ys2, yr2, own2, dpre, bt,
          ss5, sr5, xs5, xr5, zs5, zr5, own5,
          gwx, arh_in, arh, zb, yb, xb, gwo,
          load_sem, s1z, r1z, s1x, r1x, s1s, r1s, s2x, r2x, s2y, r2y,
          s4y, r4y, s4x, r4x, s5s, r5s, s5x, r5x, s5z, r5z,
          sa, ra, sbz, rbz, scy, rcy, sdx, rdx, sez, rez, sf, rf):
    row, col = lax.axis_index("row"), lax.axis_index("col")
    x, z, k = row // 16, (row // 2) % NZ, row % 2
    h, y = col // NZ, col % NZ

    def leaf(x_, z_, k_):
        return (x_ * NZ + z_) * 2 + k_

    def zdev(d):
        return (leaf(x, (z + d) % NZ, k), col)

    def ydev(d):
        return (row, h * NZ + (y + d) % NZ)

    sib = (leaf(x, z, 1 - k), col)
    xl = (leaf(1 - x, z, k), col)
    xh = (row, (1 - h) * NZ + y)
    xlh = (leaf(1 - x, z, k), (1 - h) * NZ + y)

    def copy(src, dst, ssem, rsem, dev):
        return pltpu.make_async_remote_copy(
            src_ref=src, dst_ref=dst, send_sem=ssem, recv_sem=rsem, device_id=dev, device_id_type=MESH)

    sent = []

    def send(src, dst, ssem, rsem, dev):
        cp = copy(src, dst, ssem, rsem, dev)
        cp.start()
        sent.append(cp)

    def arrive(dst, ssem, rsem):
        copy(dst, dst, ssem, rsem, sib).wait_recv()

    barrier = pltpu.get_barrier_semaphore()
    partners = [sib, xl, xh, xlh] + [zdev(d) for d in NEAR] + [ydev(d) for d in NEAR]
    for dev in partners:
        pl.semaphore_signal(barrier, inc=1, device_id=dev, device_id_type=MESH)
    load = pltpu.make_async_copy(vals_hbm, vals, load_sem)
    load.start()

    nrow = lax.rsqrt(deg[...].astype(F32))
    ncol = jnp.broadcast_to(nrow, (N, N)).T
    xg[row] = (feat[...].astype(F32) * ncol).astype(BF16)
    pl.semaphore_wait(barrier, len(partners))

    for d in FAR:
        send(xg.at[row], xg.at[row], s1z.at[d], r1z.at[d], zdev(d))
    send(xg.at[row], xg.at[row], s1x.at[0], r1x.at[0], xl)
    send(xg.at[row], xg.at[row], s1s.at[0], r1s.at[0], sib)

    def from_z(d):
        at = leaf(x, (z + NZ - d) % NZ, k)
        arrive(xg.at[at], s1z.at[d], r1z.at[d])
        send(xg.at[at], xg.at[at], s1x.at[d], r1x.at[d], xl)
        send(xg.at[at], xg.at[at], s1s.at[d], r1s.at[d], sib)

    def from_x(d):
        at = leaf(1 - x, (z + NZ - d) % NZ, k)
        arrive(xg.at[at], s1x.at[d], r1x.at[d])
        send(xg.at[at], xg.at[at], s1s.at[NZ + d], r1s.at[NZ + d], sib)

    from_z(1), from_z(7), from_x(0), from_z(2), from_z(6), from_x(1), from_x(7)
    from_z(3), from_z(5), from_x(2), from_x(6), from_z(4), from_x(3), from_x(5), from_x(4)
    for d in (0,) + NEAR:
        arrive(xg.at[leaf(x, (z + NZ - d) % NZ, 1 - k)], s1s.at[d], r1s.at[d])
    for d in (0,) + NEAR:
        arrive(xg.at[leaf(1 - x, (z + NZ - d) % NZ, 1 - k)], s1s.at[NZ + d], r1s.at[NZ + d])
    load.wait()

    def forward_turn(turn, total):
        for i in range(8):
            p = turn * 8 + i
            product = jnp.dot(vals[tab[0, PERM + p]], xg[tab[0, COLP + p]], preferred_element_type=F32)
            total = total * tab[0, KEEPF + p].astype(F32) + product
            ps[p] = total
        return total

    lax.fori_loop(0, K // 8, forward_turn, jnp.zeros((N, N), F32))

    def row_sum(at):
        return ps[tab[0, LASTR + at]] * tab[0, HASR + at].astype(F32)

    for d in FAR + (0,):
        xs2[d] = row_sum((1 - h) * NZ + (y + d) % NZ).astype(BF16)
        send(xs2.at[d], xr2.at[d], s2x.at[d], r2x.at[d], xh)
    for d in FAR + (0,):
        mine = row_sum(h * NZ + (y + d) % NZ)
        arrive(xr2.at[d], s2x.at[d], r2x.at[d])
        both = mine + xr2[d].astype(F32)
        if d:
            ys2[d] = both.astype(BF16)
            send(ys2.at[d], yr2.at[d], s2y.at[d], r2y.at[d], ydev(d))
        else:
            own2[...] = both
    smooth = own2[...]
    for d in NEAR:
        arrive(yr2.at[d], s2y.at[d], r2y.at[d])
        smooth = smooth + yr2[d].astype(F32)

    scaled = smooth * ncol
    smoothed = scaled.astype(BF16)
    gwx[...] = jnp.zeros((N, HID + N), F32)
    for c in range(HID // N):
        cs = slice(c * N, (c + 1) * N)
        pre = jnp.dot(smoothed, w[:, cs], preferred_element_type=F32) + bias[:, cs]
        square = pre * pre
        slope = 0.7978845608028654
        t = jnp.tanh(slope * (pre + 0.044715 * (square * pre)))
        half = 0.5 * (1.0 + t)
        act[:, cs] = (pre * half).astype(BF16)
        slant = half + (0.5 * slope) * pre * (1.0 - t * t) * (1.0 + (3 * 0.044715) * square)
        dp = gout[:, cs].astype(F32) * slant
        gwx[c:c + 1, HID:] = jnp.sum(dp, axis=0, keepdims=True)
        dpre[:, cs] = dp.astype(BF16)
    projected = lax.dot_general(w[...], dpre[...], (((1,), (1,)), ((), ())), preferred_element_type=F32)
    bt[col] = (projected * nrow).astype(BF16)

    for d in FAR:
        send(bt.at[col], bt.at[col], s4y.at[d], r4y.at[d], ydev(d))
    send(bt.at[col], bt.at[col], s4x.at[0], r4x.at[0], xh)
    gwx[:, :HID] = jnp.dot(scaled.T.astype(BF16), dpre[...], preferred_element_type=F32)
    send(gwx.at[pl.ds((1 - k) * 64, 64)], arh_in, sa, ra, sib)
    for d in NEAR:
        at = h * NZ + (y + NZ - d) % NZ
        arrive(bt.at[at], s4y.at[d], r4y.at[d])
        send(bt.at[at], bt.at[at], s4x.at[d], r4x.at[d], xh)
    arrive(arh_in, sa, ra)
    arh[...] = gwx[pl.ds(pl.multiple_of(k * 64, 64), 64)] + arh_in[...]
    for d in FAR:
        at = pl.multiple_of(((z + d) % NZ) * 8, 8)
        send(arh.at[pl.ds(at, 8)], zb.at[d], sbz.at[d], rbz.at[d], zdev(d))
    for d in (0,) + NEAR:
        arrive(bt.at[(1 - h) * NZ + (y + NZ - d) % NZ], s4x.at[d], r4x.at[d])

    def back_turn(turn, total):
        for i in range(8):
            p = turn * 8 + i
            product = jnp.dot(bt[tab[0, ROWK + p]], vals[p], preferred_element_type=F32)
            total = total * tab[0, KEEPB + p].astype(F32) + product
            ps[p] = total
        return total

    lax.fori_loop(0, K // 8, back_turn, jnp.zeros((N, N), F32))

    def col_sum(at):
        return ps[tab[0, LASTC + at]] * tab[0, HASC + at].astype(F32)

    for a in (1, 0):
        xa = 1 - x if a else x
        for d in range(NZ):
            ss5[a, d] = col_sum(leaf(xa, (z + d) % NZ, 1 - k)).astype(BF16)
        send(ss5.at[a], sr5.at[a], s5s.at[a], r5s.at[a], sib)
    chunk = arh[pl.ds(pl.multiple_of(z * 8, 8), 8)]
    for d in NEAR:
        arrive(zb.at[d], sbz.at[d], rbz.at[d])
        chunk = chunk + zb[d]
    yb[y] = chunk
    for d in FAR:
        send(yb.at[y], yb.at[y], scy.at[d], rcy.at[d], ydev(d))
    arrive(sr5.at[1], s5s.at[1], r5s.at[1])
    for d in FAR + (0,):
        xs5[d] = (col_sum(leaf(1 - x, (z + d) % NZ, k)) + sr5[1, d].astype(F32)).astype(BF16)
        send(xs5.at[d], xr5.at[d], s5x.at[d], r5x.at[d], xl)
    arrive(sr5.at[0], s5s.at[0], r5s.at[0])
    for d in FAR + (0,):
        mine = col_sum(leaf(x, (z + d) % NZ, k)) + sr5[0, d].astype(F32)
        arrive(xr5.at[d], s5x.at[d], r5x.at[d])
        both = mine + xr5[d].astype(F32)
        if d:
            zs5[d] = both.astype(BF16)
            send(zs5.at[d], zr5.at[d], s5z.at[d], r5z.at[d], zdev(d))
        else:
            own5[...] = both
    for d in NEAR:
        arrive(yb.at[(y + NZ - d) % NZ], scy.at[d], rcy.at[d])
    chunk = yb[0]
    for i in range(1, NZ):
        chunk = chunk + yb[i]
    me = x * 2 + h
    xb[me] = chunk
    send(xb.at[me], xb.at[me], sdx.at[0], rdx.at[0], xl)
    send(xb.at[me], xb.at[me], sdx.at[1], rdx.at[1], xh)
    send(xb.at[me], xb.at[me], sdx.at[2], rdx.at[2], xlh)
    arrive(xb.at[(1 - x) * 2 + h], sdx.at[0], rdx.at[0])
    arrive(xb.at[x * 2 + 1 - h], sdx.at[1], rdx.at[1])
    arrive(xb.at[(1 - x) * 2 + 1 - h], sdx.at[2], rdx.at[2])
    mine = pl.ds(pl.multiple_of((k * NZ + z) * 8, 8), 8)
    gwo[mine] = ((xb[0] + xb[1]) + (xb[2] + xb[3])) * (65536.0 ** -0.5)
    for d in FAR:
        send(gwo.at[mine], gwo.at[mine], sez.at[d], rez.at[d], zdev(d))
    back = own5[...]
    for d in NEAR:
        arrive(zr5.at[d], s5z.at[d], r5z.at[d])
        back = back + zr5[d].astype(F32)
    gf[...] = (back * nrow).T.astype(BF16)
    for d in NEAR:
        at = pl.ds(pl.multiple_of((k * NZ + (z + NZ - d) % NZ) * 8, 8), 8)
        arrive(gwo.at[at], sez.at[d], rez.at[d])
    ours, theirs = pl.ds(pl.multiple_of(k * 64, 64), 64), pl.ds(pl.multiple_of((1 - k) * 64, 64), 64)
    send(gwo.at[ours], gwo.at[ours], sf, rf, sib)
    arrive(gwo.at[theirs], sf, rf)
    gw[...] = gwo[:, :HID]
    for c in range(HID // N):
        gb[:, c * N:(c + 1) * N] = gwo[c:c + 1, HID:]
    for cp in sent:
        cp.wait_send()


def shards(features, degrees, proj_weight, bias, grad_out, tile_slots, tile_values):
    table = index_table(tile_slots[0, 0]).reshape(1, 256)
    vmem = pl.BlockSpec(memory_space=pltpu.VMEM)
    sem = pltpu.SemaphoreType.DMA
    tile = lambda *lead: pltpu.VMEM(lead + (N, N), BF16)
    wide = lambda *lead: pltpu.VMEM(lead + (HID + N,), F32)
    act, gw, gb, gf = pl.pallas_call(
        layer,
        name="layer",
        out_shape=(
            jax.ShapeDtypeStruct((N, HID), BF16),
            jax.ShapeDtypeStruct((N, HID), F32),
            jax.ShapeDtypeStruct((1, HID), F32),
            jax.ShapeDtypeStruct((N, N), BF16),
        ),
        in_specs=[pl.BlockSpec(memory_space=pltpu.SMEM)] + [vmem] * 5 + [pl.BlockSpec(memory_space=pl.ANY)],
        out_specs=(vmem,) * 4,
        scratch_shapes=[
            tile(K), tile(32), pltpu.VMEM((K, N, N), F32),
            tile(8), tile(8), tile(8), tile(8), pltpu.VMEM((N, N), F32),
            pltpu.VMEM((N, HID), BF16), tile(16),
            tile(2, 8), tile(2, 8), tile(8), tile(8), tile(8), tile(8), pltpu.VMEM((N, N), F32),
            wide(N), wide(64), wide(64), wide(8, 8), wide(8, 8), wide(4, 8), wide(N),
            sem, sem((8,)), sem((8,)), sem((8,)), sem((8,)), sem((16,)), sem((16,)),
            sem((8,)), sem((8,)), sem((8,)), sem((8,)),
            sem((8,)), sem((8,)), sem((8,)), sem((8,)),
            sem((2,)), sem((2,)), sem((8,)), sem((8,)), sem((8,)), sem((8,)),
            sem, sem, sem((8,)), sem((8,)), sem((8,)), sem((8,)), sem((3,)), sem((3,)),
            sem((8,)), sem((8,)), sem, sem,
        ],
        compiler_params=pltpu.CompilerParams(
            collective_id=0, has_side_effects=True, vmem_limit_bytes=40 << 20),
        cost_estimate=pl.CostEstimate(flops=3 * 10 ** 8, bytes_accessed=2 * 10 ** 6, transcendentals=65536),
    )(table, features, degrees.reshape(1, N), proj_weight, bias.reshape(1, HID), grad_out, tile_values[0, 0])
    return act, gw, gb.reshape(HID), gf


def solution(mesh):
    leaf = P(("row", "col"))
    leaf_rows = P(("row", "col"), None)
    return jax.shard_map(
        shards,
        mesh=mesh,
        in_specs=(leaf_rows, leaf, P(), P(), leaf_rows, P("row", "col", None, None), P("row", "col", None, None, None)),
        out_specs=(leaf_rows, P(), P(), leaf_rows),
        check_vma=False,
    )
```

```python
import jax
import jax.numpy as jnp
from jax import lax
from jax.experimental import pallas as pl
from jax.experimental.pallas import tpu as pltpu
from jax.sharding import PartitionSpec as P

MESH = pl.DeviceIdType.MESH
VMEM_LIMIT = 57 * 10 ** 6
BF16 = jnp.bfloat16
F32 = jnp.float32

N = 128
HID = 512
K = 32
NZ = 8
FAR = (4, 3, 5, 2, 6, 1, 7)
NEAR = (1, 7, 2, 6, 3, 5, 4)
MIXED = (2, 6, 1, 7, 4, 3, 5)
PERM, COLP, KEEPF, LASTR, HASR, ROWK, KEEPB, LASTC, HASC = range(9)


def index_table(slots):
    rows, cols = slots[0:1, :], slots[1:2, :]
    down = lax.broadcasted_iota(jnp.int32, (K, K), 0)
    along = lax.broadcasted_iota(jnp.int32, (K, K), 1)
    live = rows >= 0
    row_key = jnp.where(live, rows, 16)
    col_key = jnp.where(live, cols, 32)

    def upright(values):
        return jnp.sum(jnp.where(down == along, jnp.broadcast_to(values, (K, K)), 0), axis=1, keepdims=True)

    def place(values, where):
        return jnp.sum(jnp.where(where, jnp.broadcast_to(values, (K, K)), 0), axis=0, keepdims=True)

    def count(where):
        return jnp.sum(where.astype(jnp.int32), axis=0, keepdims=True)

    rows_up, cols_up = upright(row_key), upright(col_key)
    key_up = rows_up * K + down[:, 0:1]
    key = row_key * K + along[0:1, :]
    rank = jnp.sum((jnp.broadcast_to(key, (K, K)) < key_up).astype(jnp.int32), axis=1, keepdims=True)
    here, after = rank == along, rank + 1 == along
    row_here = place(rows_up, here)
    return (
        place(down[:, 0:1], here),
        jnp.minimum(place(cols_up, here), 31),
        (row_here == place(rows_up, after)).astype(jnp.int32),
        jnp.maximum(count(rows_up <= along) - 1, 0),
        (count(rows_up == along) > 0).astype(jnp.int32),
        jnp.minimum(row_key, 15),
        (col_key == place(cols_up, down + 1 == along)).astype(jnp.int32),
        jnp.maximum(count(cols_up <= along) - 1, 0),
        (count(cols_up == along) > 0).astype(jnp.int32),
    )


def layer(slots_hbm, feat_hbm, deg_hbm, w_hbm, bias_hbm, gout_hbm, vals_hbm,
          act_hbm, gw_hbm, gb_hbm, gf_hbm,
          act, gw, gb, gf, slots, tabv, tab, feat, deg, w, bias, gout, vals, xg, ps, xs2, xr2, ys2, yr2, own2, dpre, bt,
          ss5, sr5, xs5, xr5, zs5, zr5, own5,
          gwx, arh_in, arh, zb, yb, xb, gwo,
          load_sem, s1z, r1z, s1x, r1x, s1s, r1s, s2x, r2x, s2y, r2y,
          s4y, r4y, s4x, r4x, s5s, r5s, s5x, r5x, s5z, r5z,
          sa, ra, sbz, rbz, scy, rcy, sdx, rdx, sez, rez, sf, rf):
    row, col = lax.axis_index("row"), lax.axis_index("col")
    x, z, k = row // 16, (row // 2) % NZ, row % 2
    h, y = col // NZ, col % NZ

    def leaf(x_, z_, k_):
        return (x_ * NZ + z_) * 2 + k_

    def zdev(d):
        return (leaf(x, (z + d) % NZ, k), col)

    def ydev(d):
        return (row, h * NZ + (y + d) % NZ)

    sib = (leaf(x, z, 1 - k), col)
    xl = (leaf(1 - x, z, k), col)
    xh = (row, (1 - h) * NZ + y)
    xlh = (leaf(1 - x, z, k), (1 - h) * NZ + y)

    def copy(src, dst, ssem, rsem, dev):
        return pltpu.make_async_remote_copy(
            src_ref=src, dst_ref=dst, send_sem=ssem, recv_sem=rsem, device_id=dev, device_id_type=MESH)

    sent = []

    def send(src, dst, ssem, rsem, dev):
        cp = copy(src, dst, ssem, rsem, dev)
        cp.start()
        sent.append(cp)

    def arrive(dst, ssem, rsem):
        copy(dst, dst, ssem, rsem, sib).wait_recv()

    barrier = pltpu.get_barrier_semaphore()
    partners = [sib, xl, xh, xlh] + [zdev(d) for d in NEAR] + [ydev(d) for d in NEAR]
    for dev in partners:
        pl.semaphore_signal(barrier, inc=1, device_id=dev, device_id_type=MESH)
    loads = []
    for i, (far, here) in enumerate((
            (deg_hbm, deg), (feat_hbm, feat), (slots_hbm, slots), (vals_hbm, vals), (w_hbm, w), (bias_hbm, bias),
            (gout_hbm, gout))):
        loads.append(pltpu.make_async_copy(far, here, load_sem.at[i]))
        loads[i].start()
    loads[0].wait()
    loads[1].wait()

    nrow = lax.rsqrt(deg[...].astype(F32))
    ncol = jnp.broadcast_to(nrow, (N, N)).T
    xg[row] = (feat[...].astype(F32) * ncol).astype(BF16)
    pl.semaphore_wait(barrier, len(partners))

    for d in MIXED:
        send(xg.at[row], xg.at[row], s1z.at[d], r1z.at[d], zdev(d))
    send(xg.at[row], xg.at[row], s1x.at[0], r1x.at[0], xl)
    send(xg.at[row], xg.at[row], s1s.at[0], r1s.at[0], sib)

    loads[2].wait()
    for i, line in enumerate(index_table(slots[...])):
        tabv[i:i + 1, :K] = line
    to_scalar = pltpu.make_async_copy(tabv, tab, load_sem.at[7])
    to_scalar.start()

    def from_z(d):
        at = leaf(x, (z + NZ - d) % NZ, k)
        arrive(xg.at[at], s1z.at[d], r1z.at[d])
        send(xg.at[at], xg.at[at], s1x.at[d], r1x.at[d], xl)
        send(xg.at[at], xg.at[at], s1s.at[d], r1s.at[d], sib)

    def from_x(d):
        at = leaf(1 - x, (z + NZ - d) % NZ, k)
        arrive(xg.at[at], s1x.at[d], r1x.at[d])
        send(xg.at[at], xg.at[at], s1s.at[NZ + d], r1s.at[NZ + d], sib)

    for d in NEAR:
        from_z(d)
    for d in (0,) + NEAR:
        from_x(d)
    for d in (0,) + NEAR:
        arrive(xg.at[leaf(x, (z + NZ - d) % NZ, 1 - k)], s1s.at[d], r1s.at[d])
    for d in (0,) + NEAR:
        arrive(xg.at[leaf(1 - x, (z + NZ - d) % NZ, 1 - k)], s1s.at[NZ + d], r1s.at[NZ + d])
    to_scalar.wait()
    for i in (3, 4, 5, 6):
        loads[i].wait()

    def forward_turn(turn, total):
        for i in range(8):
            p = turn * 8 + i
            product = jnp.dot(vals[tab[PERM, p]], xg[tab[COLP, p]], preferred_element_type=F32)
            total = total * tab[KEEPF, p].astype(F32) + product
            ps[p] = total
        return total

    lax.fori_loop(0, K // 8, forward_turn, jnp.zeros((N, N), F32))

    def row_sum(at):
        return ps[tab[LASTR, at]] * tab[HASR, at].astype(F32)

    for d in FAR + (0,):
        xs2[d] = row_sum((1 - h) * NZ + (y + d) % NZ).astype(BF16)
        send(xs2.at[d], xr2.at[d], s2x.at[d], r2x.at[d], xh)
    for d in FAR + (0,):
        mine = row_sum(h * NZ + (y + d) % NZ)
        arrive(xr2.at[d], s2x.at[d], r2x.at[d])
        both = mine + xr2[d].astype(F32)
        if d:
            ys2[d] = both.astype(BF16)
            send(ys2.at[d], yr2.at[d], s2y.at[d], r2y.at[d], ydev(d))
        else:
            own2[...] = both
    smooth = own2[...]
    for d in NEAR:
        arrive(yr2.at[d], s2y.at[d], r2y.at[d])
        smooth = smooth + yr2[d].astype(F32)

    scaled = smooth * ncol
    smoothed = scaled.astype(BF16)
    gwx[...] = jnp.zeros((N, HID + N), F32)
    for c in range(HID // N):
        cs = slice(c * N, (c + 1) * N)
        pre = jnp.dot(smoothed, w[:, cs], preferred_element_type=F32) + bias[:, cs]
        square = pre * pre
        slope = 0.7978845608028654
        t = jnp.tanh(slope * (pre + 0.044715 * (square * pre)))
        half = 0.5 * (1.0 + t)
        act[:, cs] = (pre * half).astype(BF16)
        slant = half + (0.5 * slope) * pre * (1.0 - t * t) * (1.0 + (3 * 0.044715) * square)
        dp = gout[:, cs].astype(F32) * slant
        gwx[c:c + 1, HID:] = jnp.sum(dp, axis=0, keepdims=True)
        dpre[:, cs] = dp.astype(BF16)
    stores = [pltpu.make_async_copy(here, far, load_sem.at[8 + i]) for i, (here, far) in enumerate(
        ((act, act_hbm), (gf, gf_hbm), (gw, gw_hbm), (gb, gb_hbm)))]
    stores[0].start()
    projected = lax.dot_general(w[...], dpre[...], (((1,), (1,)), ((), ())), preferred_element_type=F32)
    bt[col] = (projected * nrow).astype(BF16)

    for d in MIXED:
        send(bt.at[col], bt.at[col], s4y.at[d], r4y.at[d], ydev(d))
    send(bt.at[col], bt.at[col], s4x.at[0], r4x.at[0], xh)
    gwx[:, :HID] = jnp.dot(scaled.T.astype(BF16), dpre[...], preferred_element_type=F32)
    send(gwx.at[pl.ds((1 - k) * 64, 64)], arh_in, sa, ra, sib)
    for d in NEAR:
        at = h * NZ + (y + NZ - d) % NZ
        arrive(bt.at[at], s4y.at[d], r4y.at[d])
        send(bt.at[at], bt.at[at], s4x.at[d], r4x.at[d], xh)
    arrive(arh_in, sa, ra)
    arh[...] = gwx[pl.ds(pl.multiple_of(k * 64, 64), 64)] + arh_in[...]
    for d in FAR:
        at = pl.multiple_of(((z + d) % NZ) * 8, 8)
        send(arh.at[pl.ds(at, 8)], zb.at[d], sbz.at[d], rbz.at[d], zdev(d))
    for d in (0,) + NEAR:
        arrive(bt.at[(1 - h) * NZ + (y + NZ - d) % NZ], s4x.at[d], r4x.at[d])

    def back_turn(turn, total):
        for i in range(8):
            p = turn * 8 + i
            product = jnp.dot(bt[tab[ROWK, p]], vals[p], preferred_element_type=F32)
            total = total * tab[KEEPB, p].astype(F32) + product
            ps[p] = total
        return total

    lax.fori_loop(0, K // 8, back_turn, jnp.zeros((N, N), F32))

    def col_sum(at):
        return ps[tab[LASTC, at]] * tab[HASC, at].astype(F32)

    for a in (1, 0):
        xa = 1 - x if a else x
        for d in range(NZ):
            ss5[a, d] = col_sum(leaf(xa, (z + d) % NZ, 1 - k)).astype(BF16)
        send(ss5.at[a], sr5.at[a], s5s.at[a], r5s.at[a], sib)
    chunk = arh[pl.ds(pl.multiple_of(z * 8, 8), 8)]
    for d in NEAR:
        arrive(zb.at[d], sbz.at[d], rbz.at[d])
        chunk = chunk + zb[d]
    yb[y] = chunk
    for d in FAR:
        send(yb.at[y], yb.at[y], scy.at[d], rcy.at[d], ydev(d))
    arrive(sr5.at[1], s5s.at[1], r5s.at[1])
    for d in FAR + (0,):
        xs5[d] = (col_sum(leaf(1 - x, (z + d) % NZ, k)) + sr5[1, d].astype(F32)).astype(BF16)
        send(xs5.at[d], xr5.at[d], s5x.at[d], r5x.at[d], xl)
    arrive(sr5.at[0], s5s.at[0], r5s.at[0])
    for d in FAR + (0,):
        mine = col_sum(leaf(x, (z + d) % NZ, k)) + sr5[0, d].astype(F32)
        arrive(xr5.at[d], s5x.at[d], r5x.at[d])
        both = mine + xr5[d].astype(F32)
        if d:
            zs5[d] = both.astype(BF16)
            send(zs5.at[d], zr5.at[d], s5z.at[d], r5z.at[d], zdev(d))
        else:
            own5[...] = both
    for d in NEAR:
        arrive(yb.at[(y + NZ - d) % NZ], scy.at[d], rcy.at[d])
    chunk = yb[0]
    for i in range(1, NZ):
        chunk = chunk + yb[i]
    me = x * 2 + h
    xb[me] = chunk
    send(xb.at[me], xb.at[me], sdx.at[0], rdx.at[0], xl)
    send(xb.at[me], xb.at[me], sdx.at[1], rdx.at[1], xh)
    send(xb.at[me], xb.at[me], sdx.at[2], rdx.at[2], xlh)
    arrive(xb.at[(1 - x) * 2 + h], sdx.at[0], rdx.at[0])
    arrive(xb.at[x * 2 + 1 - h], sdx.at[1], rdx.at[1])
    arrive(xb.at[(1 - x) * 2 + 1 - h], sdx.at[2], rdx.at[2])
    mine = pl.ds(pl.multiple_of((k * NZ + z) * 8, 8), 8)
    gwo[mine] = ((xb[0] + xb[1]) + (xb[2] + xb[3])) * (65536.0 ** -0.5)
    for d in FAR:
        send(gwo.at[mine], gwo.at[mine], sez.at[d], rez.at[d], zdev(d))
    back = own5[...]
    for d in NEAR:
        arrive(zr5.at[d], s5z.at[d], r5z.at[d])
        back = back + zr5[d].astype(F32)
    gf[...] = (back * nrow).T.astype(BF16)
    stores[1].start()
    for d in NEAR:
        at = pl.ds(pl.multiple_of((k * NZ + (z + NZ - d) % NZ) * 8, 8), 8)
        arrive(gwo.at[at], sez.at[d], rez.at[d])
    ours, theirs = pl.ds(pl.multiple_of(k * 64, 64), 64), pl.ds(pl.multiple_of((1 - k) * 64, 64), 64)
    send(gwo.at[ours], gwo.at[ours], sf, rf, sib)
    arrive(gwo.at[theirs], sf, rf)
    gw[...] = gwo[:, :HID]
    for c in range(HID // N):
        gb[:, c * N:(c + 1) * N] = gwo[c:c + 1, HID:]
    stores[2].start()
    stores[3].start()
    for cp in sent:
        cp.wait_send()
    for cp in stores:
        cp.wait()


def hand_over(*refs):
    sources, targets, stops, sems = refs[:4], refs[4:8], refs[8:12], refs[12]
    ins = [pltpu.make_async_copy(sources[i], stops[i], sems.at[i]) for i in range(4)]
    outs = [pltpu.make_async_copy(stops[i], targets[i], sems.at[4 + i]) for i in range(4)]
    for cp in ins:
        cp.start()
    for come, go in zip(ins, outs):
        come.wait()
        go.start()
    for cp in outs:
        cp.wait()


def shards(features, degrees, proj_weight, bias, grad_out, tile_slots, tile_values):
    anywhere = pl.BlockSpec(memory_space=pl.ANY)
    sem = pltpu.SemaphoreType.DMA
    tile = lambda *lead: pltpu.VMEM(lead + (N, N), BF16)
    wide = lambda *lead: pltpu.VMEM(lead + (HID + N,), F32)
    shapes = (
        jax.ShapeDtypeStruct((N, HID), BF16),
        jax.ShapeDtypeStruct((N, HID), F32),
        jax.ShapeDtypeStruct((1, HID), F32),
        jax.ShapeDtypeStruct((N, N), BF16),
    )
    outs = pl.pallas_call(
        layer,
        name="layer",
        out_shape=shapes,
        in_specs=[anywhere] * 7,
        out_specs=(anywhere,) * 4,
        scratch_shapes=[
            *(pltpu.VMEM(shape.shape, shape.dtype) for shape in shapes),
            pltpu.VMEM((2, K), jnp.int32), pltpu.VMEM((16, N), jnp.int32), pltpu.SMEM((16, N), jnp.int32),
            tile(), pltpu.VMEM((1, N), jnp.int32), pltpu.VMEM((N, HID), BF16), pltpu.VMEM((1, HID), F32),
            pltpu.VMEM((N, HID), BF16),
            tile(K), tile(32), pltpu.VMEM((K, N, N), F32),
            tile(8), tile(8), tile(8), tile(8), pltpu.VMEM((N, N), F32),
            pltpu.VMEM((N, HID), BF16), tile(16),
            tile(2, 8), tile(2, 8), tile(8), tile(8), tile(8), tile(8), pltpu.VMEM((N, N), F32),
            wide(N), wide(64), wide(64), wide(8, 8), wide(8, 8), wide(4, 8), wide(N),
            sem((12,)), sem((8,)), sem((8,)), sem((8,)), sem((8,)), sem((16,)), sem((16,)),
            sem((8,)), sem((8,)), sem((8,)), sem((8,)),
            sem((8,)), sem((8,)), sem((8,)), sem((8,)),
            sem((2,)), sem((2,)), sem((8,)), sem((8,)), sem((8,)), sem((8,)),
            sem, sem, sem((8,)), sem((8,)), sem((8,)), sem((8,)), sem((3,)), sem((3,)),
            sem((8,)), sem((8,)), sem, sem,
        ],
        compiler_params=pltpu.CompilerParams(
            collective_id=0, has_side_effects=True, vmem_limit_bytes=VMEM_LIMIT),
        cost_estimate=pl.CostEstimate(flops=3 * 10 ** 8, bytes_accessed=2 * 10 ** 6, transcendentals=65536),
    )(tile_slots[0, 0].T, features, degrees.reshape(1, N), proj_weight, bias.reshape(1, HID), grad_out,
      tile_values[0, 0])
    act, gw, gb, gf = pl.pallas_call(
        hand_over,
        name="hand_over",
        out_shape=shapes,
        in_specs=[anywhere] * 4,
        out_specs=(anywhere,) * 4,
        scratch_shapes=[pltpu.VMEM(shape.shape, shape.dtype) for shape in shapes] + [sem((8,))],
        compiler_params=pltpu.CompilerParams(vmem_limit_bytes=VMEM_LIMIT),
    )(*outs)
    return act, gw, gb.reshape(HID), gf


def solution(mesh):
    leaf = P(("row", "col"))
    leaf_rows = P(("row", "col"), None)
    return jax.shard_map(
        shards,
        mesh=mesh,
        in_specs=(leaf_rows, leaf, P(), P(), leaf_rows, P("row", "col", None, None), P("row", "col", None, None, None)),
        out_specs=(leaf_rows, P(), P(), leaf_rows),
        check_vma=False,
    )
```

```python
import jax
import jax.numpy as jnp
from jax import lax
from jax.experimental import pallas as pl
from jax.experimental.pallas import tpu as pltpu
from jax.sharding import PartitionSpec as P

MESH = pl.DeviceIdType.MESH
PARTS = 2
VMEM_LIMIT = 57 * 10 ** 6
BF16 = jnp.bfloat16
F32 = jnp.float32

N = 128
HID = 512
K = 32
NZ = 8
FAR = (4, 3, 5, 2, 6, 1, 7)
NEAR = (1, 7, 2, 6, 3, 5, 4)
MIXED = (2, 6, 1, 7, 4, 3, 5)
PERM, COLP, KEEPF, LASTR, HASR, ROWK, KEEPB, LASTC, HASC = range(9)


def index_table(slots):
    rows, cols = slots[0:1, :], slots[1:2, :]
    down = lax.broadcasted_iota(jnp.int32, (K, K), 0)
    along = lax.broadcasted_iota(jnp.int32, (K, K), 1)
    live = rows >= 0
    row_key = jnp.where(live, rows, 16)
    col_key = jnp.where(live, cols, 32)

    def upright(values):
        return jnp.sum(jnp.where(down == along, jnp.broadcast_to(values, (K, K)), 0), axis=1, keepdims=True)

    def place(values, where):
        return jnp.sum(jnp.where(where, jnp.broadcast_to(values, (K, K)), 0), axis=0, keepdims=True)

    def count(where):
        return jnp.sum(where.astype(jnp.int32), axis=0, keepdims=True)

    rows_up, cols_up = upright(row_key), upright(col_key)
    key_up = rows_up * K + down[:, 0:1]
    key = row_key * K + along[0:1, :]
    rank = jnp.sum((jnp.broadcast_to(key, (K, K)) < key_up).astype(jnp.int32), axis=1, keepdims=True)
    here, after = rank == along, rank + 1 == along
    row_here = place(rows_up, here)
    col_here = jnp.minimum(place(cols_up, here), 31)
    spots = (col_here & 1) * 16 + lax.shift_right_logical(col_here, 1)
    return (
        place(down[:, 0:1], here),
        spots,
        (row_here == place(rows_up, after)).astype(jnp.int32),
        jnp.maximum(count(rows_up <= along) - 1, 0),
        (count(rows_up == along) > 0).astype(jnp.int32),
        jnp.minimum(row_key, 15),
        (col_key == place(cols_up, down + 1 == along)).astype(jnp.int32),
        jnp.maximum(count(cols_up <= along) - 1, 0),
        (count(cols_up == along) > 0).astype(jnp.int32),
    )


def layer(slots_hbm, feat_hbm, deg_hbm, w_hbm, bias_hbm, gout_hbm, vals_hbm,
          act_hbm, gw_hbm, gb_hbm, gf_hbm,
          act, gw, gb, gf, slots, tabv, tab, feat, deg, w, bias, gout, vals,
          xg0, xg1, ps, xs2, xr2, ys2, yr2, dpre, bt0, bt1,
          ss5, sr5, xs5, xr5, zs5, zr5,
          gwx, arh_in, arh, zb, yb, xb, gwo,
          load_sem, s1z, r1z, s1x, r1x, s1s, r1s, s2x, r2x, s2y, r2y,
          s4y, r4y, s4x, r4x, s5s, r5s, s5x, r5x, s5z, r5z,
          sa, ra, sbz, rbz, scy, rcy, sdx, rdx, sez, rez, sf, rf):
    row, col = lax.axis_index("row"), lax.axis_index("col")
    x, z, k = row // 16, (row // 2) % NZ, row % 2
    h, y = col // NZ, col % NZ
    xg, bt = (xg0, xg1), (bt0, bt1)
    part = [pl.ds(q * (N // PARTS), N // PARTS) for q in range(PARTS)]

    def leaf(x_, z_, k_):
        return (x_ * NZ + z_) * 2 + k_

    def spot(x_, z_, k_):
        return k_ * 16 + x_ * NZ + z_

    def behind(at, d):
        return (at + NZ - d) % NZ

    def zdev(d):
        return (leaf(x, (z + d) % NZ, k), col)

    def ydev(d):
        return (row, h * NZ + (y + d) % NZ)

    sib = (leaf(x, z, 1 - k), col)
    xl = (leaf(1 - x, z, k), col)
    xh = (row, (1 - h) * NZ + y)
    xlh = (leaf(1 - x, z, k), (1 - h) * NZ + y)

    def copy(src, dst, ssem, rsem, dev):
        return pltpu.make_async_remote_copy(
            src_ref=src, dst_ref=dst, send_sem=ssem, recv_sem=rsem, device_id=dev, device_id_type=MESH)

    sent = []

    def send(src, dst, ssem, rsem, dev):
        cp = copy(src, dst, ssem, rsem, dev)
        cp.start()
        sent.append(cp)

    def arrive(dst, ssem, rsem):
        copy(dst, dst, ssem, rsem, sib).wait_recv()

    barrier = pltpu.get_barrier_semaphore()
    partners = [sib, xl, xh, xlh] + [zdev(d) for d in NEAR] + [ydev(d) for d in NEAR]
    for dev in partners:
        pl.semaphore_signal(barrier, inc=1, device_id=dev, device_id_type=MESH)
    loads = []
    for i, (far, here) in enumerate((
            (deg_hbm, deg), (feat_hbm, feat), (slots_hbm, slots), (vals_hbm, vals), (w_hbm, w), (bias_hbm, bias),
            (gout_hbm, gout))):
        loads.append(pltpu.make_async_copy(far, here, load_sem.at[i]))
        loads[i].start()
    stores = [pltpu.make_async_copy(here, far, load_sem.at[8 + i]) for i, (here, far) in enumerate(
        ((act, act_hbm), (gf, gf_hbm), (gw, gw_hbm), (gb, gb_hbm)))]
    loads[0].wait()
    loads[1].wait()

    nrow = lax.rsqrt(deg[...].astype(F32))
    mine = spot(x, z, k)
    scaled = (feat[...].astype(F32).T * nrow).astype(BF16)
    for q in range(PARTS):
        xg[q][mine] = scaled[q * (N // PARTS):(q + 1) * (N // PARTS)]
    pl.semaphore_wait(barrier, len(partners))

    for q in range(PARTS):
        at = xg[q].at[mine]
        for d in MIXED:
            send(at, at, s1z.at[q, d], r1z.at[q, d], zdev(d))
        send(at, at, s1x.at[q, 0], r1x.at[q, 0], xl)

    loads[2].wait()
    for i, line in enumerate(index_table(slots[...])):
        tabv[i:i + 1, :K] = line
    to_scalar = pltpu.make_async_copy(tabv, tab, load_sem.at[7])
    to_scalar.start()

    def half_to_sib(q, i, x_):
        at = xg[q].at[pl.ds(spot(x_, 0, k), NZ)]
        send(at, at, s1s.at[q, i], r1s.at[q, i], sib)

    def half_from_sib(q, i, x_):
        arrive(xg[q].at[pl.ds(spot(x_, 0, 1 - k), NZ)], s1s.at[q, i], r1s.at[q, i])

    for q in range(PARTS):
        for d in NEAR:
            at = xg[q].at[spot(x, behind(z, d), k)]
            arrive(at, s1z.at[q, d], r1z.at[q, d])
            send(at, at, s1x.at[q, d], r1x.at[q, d], xl)
        half_to_sib(q, 0, x)
    to_scalar.wait()
    loads[3].wait()

    def row_sum(at, q):
        return ps[tab[LASTR, at], part[q]] * tab[HASR, at].astype(F32)

    for q in range(PARTS):
        for d in (0,) + NEAR:
            arrive(xg[q].at[spot(1 - x, behind(z, d), k)], s1x.at[q, d], r1x.at[q, d])
        half_to_sib(q, 1, 1 - x)
        half_from_sib(q, 0, x)
        half_from_sib(q, 1, 1 - x)

        def forward_turn(turn, total):
            for i in range(8):
                p = turn * 8 + i
                product = lax.dot_general(xg[q][tab[COLP, p]], vals[tab[PERM, p]],
                                          (((1,), (1,)), ((), ())), preferred_element_type=F32)
                total = total * tab[KEEPF, p].astype(F32) + product
                ps[p, part[q]] = total
            return total

        lax.fori_loop(0, K // 8, forward_turn, jnp.zeros((N // PARTS, N), F32))
        for d in FAR + (0,):
            xs2[d, part[q]] = row_sum((1 - h) * NZ + (y + d) % NZ, q).astype(BF16)
            send(xs2.at[d, part[q]], xr2.at[d, part[q]], s2x.at[q, d], r2x.at[q, d], xh)
    smooth = [None] * PARTS
    for q in range(PARTS):
        for d in FAR + (0,):
            own = row_sum(h * NZ + (y + d) % NZ, q)
            arrive(xr2.at[d, part[q]], s2x.at[q, d], r2x.at[q, d])
            both = own + xr2[d, part[q]].astype(F32)
            if d:
                ys2[d, part[q]] = both.astype(BF16)
                send(ys2.at[d, part[q]], yr2.at[d, part[q]], s2y.at[q, d], r2y.at[q, d], ydev(d))
            else:
                smooth[q] = both
    for i in (4, 5, 6):
        loads[i].wait()
    for q in range(PARTS):
        for d in NEAR:
            arrive(yr2.at[d, part[q]], s2y.at[q, d], r2y.at[q, d])
            smooth[q] = smooth[q] + yr2[d, part[q]].astype(F32)

    smoothed = (jnp.concatenate(smooth, axis=0) * nrow).astype(BF16)
    gwx[...] = jnp.zeros((N, HID + N), F32)
    for c in range(HID // N):
        cs = slice(c * N, (c + 1) * N)
        pre = lax.dot_general(smoothed, w[:, cs], (((0,), (0,)), ((), ())), preferred_element_type=F32) + bias[:, cs]
        square = pre * pre
        slope = 0.7978845608028654
        t = jnp.tanh(slope * (pre + 0.044715 * (square * pre)))
        half = 0.5 * (1.0 + t)
        act[:, cs] = (pre * half).astype(BF16)
        slant = half + (0.5 * slope) * pre * (1.0 - t * t) * (1.0 + (3 * 0.044715) * square)
        dp = gout[:, cs].astype(F32) * slant
        gwx[c:c + 1, HID:] = jnp.sum(dp, axis=0, keepdims=True)
        dpre[:, cs] = dp.astype(BF16)
    projected = lax.dot_general(w[...], dpre[...], (((1,), (1,)), ((), ())), preferred_element_type=F32)
    back_in = (projected * nrow).astype(BF16)
    for q in range(PARTS):
        bt[q][col] = back_in[q * (N // PARTS):(q + 1) * (N // PARTS)]

    for q in range(PARTS):
        at = bt[q].at[col]
        for d in MIXED:
            send(at, at, s4y.at[q, d], r4y.at[q, d], ydev(d))
        send(at, at, s4x.at[q, 0], r4x.at[q, 0], xh)
    stores[0].start()
    gwx[:, :HID] = jnp.dot(smoothed, dpre[...], preferred_element_type=F32)
    ours, theirs = pl.ds(pl.multiple_of(k * 64, 64), 64), pl.ds(pl.multiple_of((1 - k) * 64, 64), 64)
    send(gwx.at[theirs], arh_in, sa, ra, sib)
    arrive(arh_in, sa, ra)
    arh[...] = gwx[ours] + arh_in[...]
    for d in FAR:
        at = pl.multiple_of(((z + d) % NZ) * 8, 8)
        send(arh.at[pl.ds(at, 8)], zb.at[d], sbz.at[d], rbz.at[d], zdev(d))
    for q in range(PARTS):
        for d in NEAR:
            at = bt[q].at[h * NZ + behind(y, d)]
            arrive(at, s4y.at[q, d], r4y.at[q, d])
            send(at, at, s4x.at[q, d], r4x.at[q, d], xh)
    chunk = arh[pl.ds(pl.multiple_of(z * 8, 8), 8)]
    for d in NEAR:
        arrive(zb.at[d], sbz.at[d], rbz.at[d])
        chunk = chunk + zb[d]
    yb[y] = chunk
    for d in FAR:
        send(yb.at[y], yb.at[y], scy.at[d], rcy.at[d], ydev(d))

    def col_sum(at, q):
        return ps[tab[LASTC, at], part[q]] * tab[HASC, at].astype(F32)

    def to_x(q):
        arrive(sr5.at[1, :, part[q]], s5s.at[q, 1], r5s.at[q, 1])
        for d in FAR + (0,):
            xs5[d, part[q]] = (col_sum(leaf(1 - x, (z + d) % NZ, k), q) + sr5[1, d, part[q]].astype(F32)).astype(BF16)
            send(xs5.at[d, part[q]], xr5.at[d, part[q]], s5x.at[q, d], r5x.at[q, d], xl)

    for q in range(PARTS):
        for d in (0,) + NEAR:
            arrive(bt[q].at[(1 - h) * NZ + behind(y, d)], s4x.at[q, d], r4x.at[q, d])
        if q:
            to_x(q - 1)

        def back_turn(turn, total):
            for i in range(8):
                p = turn * 8 + i
                product = jnp.dot(bt[q][tab[ROWK, p]], vals[p], preferred_element_type=F32)
                total = total * tab[KEEPB, p].astype(F32) + product
                ps[p, part[q]] = total
            return total

        lax.fori_loop(0, K // 8, back_turn, jnp.zeros((N // PARTS, N), F32))
        for a in (1, 0):
            xa = 1 - x if a else x
            for d in range(NZ):
                ss5[a, d, part[q]] = col_sum(leaf(xa, (z + d) % NZ, 1 - k), q).astype(BF16)
            send(ss5.at[a, :, part[q]], sr5.at[a, :, part[q]], s5s.at[q, a], r5s.at[q, a], sib)
    to_x(PARTS - 1)
    for d in NEAR:
        arrive(yb.at[behind(y, d)], scy.at[d], rcy.at[d])
    chunk = yb[0]
    for i in range(1, NZ):
        chunk = chunk + yb[i]
    me = x * 2 + h
    xb[me] = chunk
    send(xb.at[me], xb.at[me], sdx.at[0], rdx.at[0], xl)
    send(xb.at[me], xb.at[me], sdx.at[1], rdx.at[1], xh)
    send(xb.at[me], xb.at[me], sdx.at[2], rdx.at[2], xlh)
    back = [None] * PARTS
    for q in range(PARTS):
        arrive(sr5.at[0, :, part[q]], s5s.at[q, 0], r5s.at[q, 0])
        for d in FAR + (0,):
            own = col_sum(leaf(x, (z + d) % NZ, k), q) + sr5[0, d, part[q]].astype(F32)
            arrive(xr5.at[d, part[q]], s5x.at[q, d], r5x.at[q, d])
            both = own + xr5[d, part[q]].astype(F32)
            if d:
                zs5[d, part[q]] = both.astype(BF16)
                send(zs5.at[d, part[q]], zr5.at[d, part[q]], s5z.at[q, d], r5z.at[q, d], zdev(d))
            else:
                back[q] = both
    arrive(xb.at[(1 - x) * 2 + h], sdx.at[0], rdx.at[0])
    arrive(xb.at[x * 2 + 1 - h], sdx.at[1], rdx.at[1])
    arrive(xb.at[(1 - x) * 2 + 1 - h], sdx.at[2], rdx.at[2])
    rows = pl.ds(pl.multiple_of((k * NZ + z) * 8, 8), 8)
    gwo[rows] = ((xb[0] + xb[1]) + (xb[2] + xb[3])) * (65536.0 ** -0.5)
    for d in FAR:
        send(gwo.at[rows], gwo.at[rows], sez.at[d], rez.at[d], zdev(d))
    for q in range(PARTS):
        for d in NEAR:
            arrive(zr5.at[d, part[q]], s5z.at[q, d], r5z.at[q, d])
            back[q] = back[q] + zr5[d, part[q]].astype(F32)
    gf[...] = (jnp.concatenate(back, axis=0) * nrow).T.astype(BF16)
    stores[1].start()
    for d in NEAR:
        at = pl.ds(pl.multiple_of((k * NZ + behind(z, d)) * 8, 8), 8)
        arrive(gwo.at[at], sez.at[d], rez.at[d])
    send(gwo.at[ours], gwo.at[ours], sf, rf, sib)
    arrive(gwo.at[theirs], sf, rf)
    gw[...] = gwo[:, :HID]
    for c in range(HID // N):
        gb[:, c * N:(c + 1) * N] = gwo[c:c + 1, HID:]
    stores[2].start()
    stores[3].start()
    for cp in sent:
        cp.wait_send()
    for cp in stores:
        cp.wait()


def hand_over(*refs):
    sources, targets, stops, sems = refs[:4], refs[4:8], refs[8:12], refs[12]
    ins = [pltpu.make_async_copy(sources[i], stops[i], sems.at[i]) for i in range(4)]
    outs = [pltpu.make_async_copy(stops[i], targets[i], sems.at[4 + i]) for i in range(4)]
    for cp in ins:
        cp.start()
    for come, go in zip(ins, outs):
        come.wait()
        go.start()
    for cp in outs:
        cp.wait()


def shards(features, degrees, proj_weight, bias, grad_out, tile_slots, tile_values):
    anywhere = pl.BlockSpec(memory_space=pl.ANY)
    sem = pltpu.SemaphoreType.DMA
    tile = lambda *lead: pltpu.VMEM(lead + (N, N), BF16)
    flat = lambda count: pltpu.VMEM((count, N // PARTS, N), BF16)
    wide = lambda *lead: pltpu.VMEM(lead + (HID + N,), F32)
    shapes = (
        jax.ShapeDtypeStruct((N, HID), BF16),
        jax.ShapeDtypeStruct((N, HID), F32),
        jax.ShapeDtypeStruct((1, HID), F32),
        jax.ShapeDtypeStruct((N, N), BF16),
    )
    outs = pl.pallas_call(
        layer,
        name="layer",
        out_shape=shapes,
        in_specs=[anywhere] * 7,
        out_specs=(anywhere,) * 4,
        scratch_shapes=[
            *(pltpu.VMEM(shape.shape, shape.dtype) for shape in shapes),
            pltpu.VMEM((2, K), jnp.int32), pltpu.VMEM((16, N), jnp.int32), pltpu.SMEM((16, N), jnp.int32),
            tile(), pltpu.VMEM((1, N), jnp.int32), pltpu.VMEM((N, HID), BF16), pltpu.VMEM((1, HID), F32),
            pltpu.VMEM((N, HID), BF16),
            tile(K), flat(32), flat(32), pltpu.VMEM((K, N, N), F32),
            tile(8), tile(8), tile(8), tile(8), pltpu.VMEM((N, HID), BF16), flat(16), flat(16),
            tile(2, 8), tile(2, 8), tile(8), tile(8), tile(8), tile(8),
            wide(N), wide(64), wide(64), wide(8, 8), wide(8, 8), wide(4, 8), wide(N),
            sem((12,)), *[sem((PARTS, 8))] * 4, *[sem((PARTS, 2))] * 2, *[sem((PARTS, 8))] * 8,
            *[sem((PARTS, 2))] * 2, *[sem((PARTS, 8))] * 4,
            sem, sem, sem((8,)), sem((8,)), sem((8,)), sem((8,)), sem((3,)), sem((3,)),
            sem((8,)), sem((8,)), sem, sem,
        ],
        compiler_params=pltpu.CompilerParams(
            collective_id=0, has_side_effects=True, vmem_limit_bytes=VMEM_LIMIT),
        cost_estimate=pl.CostEstimate(flops=3 * 10 ** 8, bytes_accessed=2 * 10 ** 6, transcendentals=65536),
    )(tile_slots[0, 0].T, features, degrees.reshape(1, N), proj_weight, bias.reshape(1, HID), grad_out,
      tile_values[0, 0])
    act, gw, gb, gf = pl.pallas_call(
        hand_over,
        name="hand_over",
        out_shape=shapes,
        in_specs=[anywhere] * 4,
        out_specs=(anywhere,) * 4,
        scratch_shapes=[pltpu.VMEM(shape.shape, shape.dtype) for shape in shapes] + [sem((8,))],
        compiler_params=pltpu.CompilerParams(vmem_limit_bytes=VMEM_LIMIT),
    )(*outs)
    return act, gw, gb.reshape(HID), gf


def solution(mesh):
    leaf = P(("row", "col"))
    leaf_rows = P(("row", "col"), None)
    return jax.shard_map(
        shards,
        mesh=mesh,
        in_specs=(leaf_rows, leaf, P(), P(), leaf_rows, P("row", "col", None, None), P("row", "col", None, None, None)),
        out_specs=(leaf_rows, P(), P(), leaf_rows),
        check_vma=False,
    )
```

```python
import jax
import jax.numpy as jnp
from jax import lax
from jax.experimental import pallas as pl
from jax.experimental.pallas import tpu as pltpu
from jax.sharding import PartitionSpec as P

MESH = pl.DeviceIdType.MESH
PARTS = 2
VMEM_LIMIT = 57 * 10 ** 6
BF16 = jnp.bfloat16
F32 = jnp.float32

N = 128
HID = 512
WIDE = HID // 2 + N
K = 32
NZ = 8
FAR = (4, 3, 5, 2, 6, 1, 7)
NEAR = (1, 7, 2, 6, 3, 5, 4)
MIXED = (2, 6, 1, 7, 4, 3, 5)
PERM, COLP, KEEPF, LASTR, HASR, ROWK, KEEPB, LASTC, HASC = range(9)


def index_table(slots):
    rows, cols = slots[0:1, :], slots[1:2, :]
    down = lax.broadcasted_iota(jnp.int32, (K, K), 0)
    along = lax.broadcasted_iota(jnp.int32, (K, K), 1)
    live = rows >= 0
    row_key = jnp.where(live, rows, 16)
    col_key = jnp.where(live, cols, 32)

    def upright(values):
        return jnp.sum(jnp.where(down == along, jnp.broadcast_to(values, (K, K)), 0), axis=1, keepdims=True)

    def place(values, where):
        return jnp.sum(jnp.where(where, jnp.broadcast_to(values, (K, K)), 0), axis=0, keepdims=True)

    def count(where):
        return jnp.sum(where.astype(jnp.int32), axis=0, keepdims=True)

    rows_up, cols_up = upright(row_key), upright(col_key)
    key_up = rows_up * K + down[:, 0:1]
    key = row_key * K + along[0:1, :]
    rank = jnp.sum((jnp.broadcast_to(key, (K, K)) < key_up).astype(jnp.int32), axis=1, keepdims=True)
    here, after = rank == along, rank + 1 == along
    row_here = place(rows_up, here)
    col_here = jnp.minimum(place(cols_up, here), 31)
    spots = (col_here & 1) * 16 + lax.shift_right_logical(col_here, 1)
    return (
        place(down[:, 0:1], here),
        spots,
        (row_here == place(rows_up, after)).astype(jnp.int32),
        jnp.maximum(count(rows_up <= along) - 1, 0),
        (count(rows_up == along) > 0).astype(jnp.int32),
        jnp.minimum(row_key, 15),
        (col_key == place(cols_up, down + 1 == along)).astype(jnp.int32),
        jnp.maximum(count(cols_up <= along) - 1, 0),
        (count(cols_up == along) > 0).astype(jnp.int32),
    )


def layer(slots_hbm, feat_hbm, deg_hbm, w_hbm, bias_hbm, gout_hbm, vals_hbm,
          act_hbm, gw_hbm, gb_hbm, gf_hbm,
          act, gw, gb, gf, slots, tabv, tab, feat, deg, w, bias, gout, vals,
          xg0, xg1, ps, xs2, xr2, ys2, yr2, dpre, bt0, bt1,
          ss5, sr5, xs5, xr5, zs5, zr5,
          gwx, arh_in, arh, zs, zb, yb, xb, gwo,
          load_sem, s1z, r1z, s1x, r1x, s1s, r1s, s2x, r2x, s2y, r2y,
          s4y, r4y, s4x, r4x, s5s, r5s, s5x, r5x, s5z, r5z,
          sa, ra, sbz, rbz, scy, rcy, sdx, rdx, sez, rez, sf, rf):
    row, col = lax.axis_index("row"), lax.axis_index("col")
    x, z, k = row // 16, (row // 2) % NZ, row % 2
    h, y = col // NZ, col % NZ
    xg, bt = (xg0, xg1), (bt0, bt1)
    part = [pl.ds(q * (N // PARTS), N // PARTS) for q in range(PARTS)]

    def leaf(x_, z_, k_):
        return (x_ * NZ + z_) * 2 + k_

    def spot(x_, z_, k_):
        return k_ * 16 + x_ * NZ + z_

    def behind(at, d):
        return (at + NZ - d) % NZ

    def zdev(d):
        return (leaf(x, (z + d) % NZ, k), col)

    def ydev(d):
        return (row, h * NZ + (y + d) % NZ)

    sib = (leaf(x, z, 1 - k), col)
    xl = (leaf(1 - x, z, k), col)
    xh = (row, (1 - h) * NZ + y)
    xlh = (leaf(1 - x, z, k), (1 - h) * NZ + y)

    def copy(src, dst, ssem, rsem, dev):
        return pltpu.make_async_remote_copy(
            src_ref=src, dst_ref=dst, send_sem=ssem, recv_sem=rsem, device_id=dev, device_id_type=MESH)

    sent = {1: [], 2: [], 4: [], 5: []}

    def send(phase, src, dst, ssem, rsem, dev):
        cp = copy(src, dst, ssem, rsem, dev)
        cp.start()
        sent[phase].append(cp)

    def settle(phase):
        for cp in sent[phase]:
            cp.wait_send()

    def arrive(dst, ssem, rsem):
        copy(dst, dst, ssem, rsem, sib).wait_recv()

    barrier = pltpu.get_barrier_semaphore()
    partners = [sib, xl, xh, xlh] + [zdev(d) for d in NEAR] + [ydev(d) for d in NEAR]
    for dev in partners:
        pl.semaphore_signal(barrier, inc=1, device_id=dev, device_id_type=MESH)
    loads = []
    for i, (far, here) in enumerate((
            (deg_hbm, deg), (feat_hbm, feat), (slots_hbm, slots), (vals_hbm, vals), (w_hbm, w), (bias_hbm, bias),
            (gout_hbm, gout))):
        loads.append(pltpu.make_async_copy(far, here, load_sem.at[i]))
        loads[i].start()
    stores = [pltpu.make_async_copy(here, far, load_sem.at[8 + i]) for i, (here, far) in enumerate(
        ((act, act_hbm), (gf, gf_hbm), (gw, gw_hbm), (gb, gb_hbm)))]
    loads[0].wait()
    loads[1].wait()

    nrow = lax.rsqrt(deg[...].astype(F32))
    mine = spot(x, z, k)
    scaled = (feat[...].astype(F32).T * nrow).astype(BF16)
    for q in range(PARTS):
        xg[q][mine] = scaled[q * (N // PARTS):(q + 1) * (N // PARTS)]
    pl.semaphore_wait(barrier, len(partners))

    for q in range(PARTS):
        at = xg[q].at[mine]
        for d in MIXED:
            send(1, at, at, s1z.at[q, d], r1z.at[q, d], zdev(d))
        send(1, at, at, s1x.at[q, 0], r1x.at[q, 0], xl)

    loads[2].wait()
    for i, line in enumerate(index_table(slots[...])):
        tabv[i:i + 1, :K] = line
    to_scalar = pltpu.make_async_copy(tabv, tab, load_sem.at[7])
    to_scalar.start()

    def half_to_sib(q, i, x_):
        at = xg[q].at[pl.ds(spot(x_, 0, k), NZ)]
        send(1, at, at, s1s.at[q, i], r1s.at[q, i], sib)

    def half_from_sib(q, i, x_):
        arrive(xg[q].at[pl.ds(spot(x_, 0, 1 - k), NZ)], s1s.at[q, i], r1s.at[q, i])

    for q in range(PARTS):
        for d in NEAR:
            at = xg[q].at[spot(x, behind(z, d), k)]
            arrive(at, s1z.at[q, d], r1z.at[q, d])
            send(1, at, at, s1x.at[q, d], r1x.at[q, d], xl)
        half_to_sib(q, 0, x)
    to_scalar.wait()
    loads[3].wait()

    def row_sum(at, q):
        return ps[tab[LASTR, at], part[q]] * tab[HASR, at].astype(F32)

    for q in range(PARTS):
        for d in (0,) + NEAR:
            arrive(xg[q].at[spot(1 - x, behind(z, d), k)], s1x.at[q, d], r1x.at[q, d])
        half_to_sib(q, 1, 1 - x)
        half_from_sib(q, 0, x)
        half_from_sib(q, 1, 1 - x)

        def forward_turn(turn, total):
            for i in range(8):
                p = turn * 8 + i
                product = lax.dot_general(xg[q][tab[COLP, p]], vals[tab[PERM, p]],
                                          (((1,), (1,)), ((), ())), preferred_element_type=F32)
                total = total * tab[KEEPF, p].astype(F32) + product
                ps[p, part[q]] = total
            return total

        lax.fori_loop(0, K // 8, forward_turn, jnp.zeros((N // PARTS, N), F32))
        for d in FAR + (0,):
            xs2[d, part[q]] = row_sum((1 - h) * NZ + (y + d) % NZ, q).astype(BF16)
            send(2, xs2.at[d, part[q]], xr2.at[d, part[q]], s2x.at[q, d], r2x.at[q, d], xh)
    settle(1)
    smooth = [None] * PARTS
    for q in range(PARTS):
        for d in FAR + (0,):
            own = row_sum(h * NZ + (y + d) % NZ, q)
            arrive(xr2.at[d, part[q]], s2x.at[q, d], r2x.at[q, d])
            both = own + xr2[d, part[q]].astype(F32)
            if d:
                ys2[d, part[q]] = both.astype(BF16)
                send(2, ys2.at[d, part[q]], yr2.at[d, part[q]], s2y.at[q, d], r2y.at[q, d], ydev(d))
            else:
                smooth[q] = both
    for i in (4, 5, 6):
        loads[i].wait()
    for q in range(PARTS):
        for d in NEAR:
            arrive(yr2.at[d, part[q]], s2y.at[q, d], r2y.at[q, d])
            smooth[q] = smooth[q] + yr2[d, part[q]].astype(F32)

    smoothed = (jnp.concatenate(smooth, axis=0) * nrow).astype(BF16)
    gwx[...] = jnp.zeros((2, N, WIDE), F32)
    for c in range(HID // N):
        cs = slice(c * N, (c + 1) * N)
        pre = lax.dot_general(smoothed, w[:, cs], (((0,), (0,)), ((), ())), preferred_element_type=F32) + bias[:, cs]
        square = pre * pre
        slope = 0.7978845608028654
        t = jnp.tanh(slope * (pre + 0.044715 * (square * pre)))
        half = 0.5 * (1.0 + t)
        act[:, cs] = (pre * half).astype(BF16)
        slant = half + (0.5 * slope) * pre * (1.0 - t * t) * (1.0 + (3 * 0.044715) * square)
        dp = gout[:, cs].astype(F32) * slant
        gwx[c // 2, c % 2:c % 2 + 1, HID // 2:] = jnp.sum(dp, axis=0, keepdims=True)
        dpre[:, cs] = dp.astype(BF16)
    projected = lax.dot_general(w[...], dpre[...], (((1,), (1,)), ((), ())), preferred_element_type=F32)
    back_in = (projected * nrow).astype(BF16)
    for q in range(PARTS):
        bt[q][col] = back_in[q * (N // PARTS):(q + 1) * (N // PARTS)]

    for q in range(PARTS):
        at = bt[q].at[col]
        for d in MIXED:
            send(4, at, at, s4y.at[q, d], r4y.at[q, d], ydev(d))
        send(4, at, at, s4x.at[q, 0], r4x.at[q, 0], xh)
    stores[0].start()
    for i in range(2):
        cs = slice(i * HID // 2, (i + 1) * HID // 2)
        gwx[i, :, :HID // 2] = jnp.dot(smoothed, dpre[:, cs], preferred_element_type=F32)
    ours, theirs = pl.ds(pl.multiple_of(k * 64, 64), 64), pl.ds(pl.multiple_of((1 - k) * 64, 64), 64)
    send(4, gwx.at[:, theirs], arh_in, sa, ra, sib)
    arrive(arh_in, sa, ra)
    arh[...] = gwx[:, ours] + arh_in[...]

    def eighth(at):
        return arh[at % 2, pl.ds(pl.multiple_of(at // 2 * 16, 16), 16)]

    for d in FAR:
        zs[d] = eighth((z + d) % NZ).astype(BF16)
        send(4, zs.at[d], zb.at[d], sbz.at[d], rbz.at[d], zdev(d))
    settle(2)
    for q in range(PARTS):
        for d in NEAR:
            at = bt[q].at[h * NZ + behind(y, d)]
            arrive(at, s4y.at[q, d], r4y.at[q, d])
            send(4, at, at, s4x.at[q, d], r4x.at[q, d], xh)
    chunk = eighth(z)
    for d in NEAR:
        arrive(zb.at[d], sbz.at[d], rbz.at[d])
        chunk = chunk + zb[d].astype(F32)
    yb[y] = chunk.astype(BF16)
    for d in FAR:
        send(4, yb.at[y], yb.at[y], scy.at[d], rcy.at[d], ydev(d))

    def col_sum(at, q):
        return ps[tab[LASTC, at], part[q]] * tab[HASC, at].astype(F32)

    def to_x(q):
        arrive(sr5.at[1, :, part[q]], s5s.at[q, 1], r5s.at[q, 1])
        for d in FAR + (0,):
            xs5[d, part[q]] = (col_sum(leaf(1 - x, (z + d) % NZ, k), q) + sr5[1, d, part[q]].astype(F32)).astype(BF16)
            send(5, xs5.at[d, part[q]], xr5.at[d, part[q]], s5x.at[q, d], r5x.at[q, d], xl)

    for q in range(PARTS):
        for d in (0,) + NEAR:
            arrive(bt[q].at[(1 - h) * NZ + behind(y, d)], s4x.at[q, d], r4x.at[q, d])
        if q:
            to_x(q - 1)

        def back_turn(turn, total):
            for i in range(8):
                p = turn * 8 + i
                product = jnp.dot(bt[q][tab[ROWK, p]], vals[p], preferred_element_type=F32)
                total = total * tab[KEEPB, p].astype(F32) + product
                ps[p, part[q]] = total
            return total

        lax.fori_loop(0, K // 8, back_turn, jnp.zeros((N // PARTS, N), F32))
        for a in (1, 0):
            xa = 1 - x if a else x
            for d in range(NZ):
                ss5[a, d, part[q]] = col_sum(leaf(xa, (z + d) % NZ, 1 - k), q).astype(BF16)
            send(5, ss5.at[a, :, part[q]], sr5.at[a, :, part[q]], s5s.at[q, a], r5s.at[q, a], sib)
    for d in NEAR:
        arrive(yb.at[behind(y, d)], scy.at[d], rcy.at[d])
    chunk = yb[0].astype(F32)
    for i in range(1, NZ):
        chunk = chunk + yb[i].astype(F32)
    me = x * 2 + h
    xb[me] = chunk
    send(5, xb.at[me], xb.at[me], sdx.at[0], rdx.at[0], xl)
    send(5, xb.at[me], xb.at[me], sdx.at[1], rdx.at[1], xh)
    send(5, xb.at[me], xb.at[me], sdx.at[2], rdx.at[2], xlh)
    to_x(PARTS - 1)
    settle(4)
    back = [None] * PARTS
    for q in range(PARTS):
        arrive(sr5.at[0, :, part[q]], s5s.at[q, 0], r5s.at[q, 0])
        for d in FAR + (0,):
            own = col_sum(leaf(x, (z + d) % NZ, k), q) + sr5[0, d, part[q]].astype(F32)
            arrive(xr5.at[d, part[q]], s5x.at[q, d], r5x.at[q, d])
            both = own + xr5[d, part[q]].astype(F32)
            if d:
                zs5[d, part[q]] = both.astype(BF16)
                send(5, zs5.at[d, part[q]], zr5.at[d, part[q]], s5z.at[q, d], r5z.at[q, d], zdev(d))
            else:
                back[q] = both
        if q == 0:
            arrive(xb.at[(1 - x) * 2 + h], sdx.at[0], rdx.at[0])
            arrive(xb.at[x * 2 + 1 - h], sdx.at[1], rdx.at[1])
            arrive(xb.at[(1 - x) * 2 + 1 - h], sdx.at[2], rdx.at[2])
            gwo[k * NZ + z] = (((xb[0] + xb[1]) + (xb[2] + xb[3])) * (65536.0 ** -0.5)).astype(BF16)
            for d in FAR:
                send(5, gwo.at[k * NZ + z], gwo.at[k * NZ + z], sez.at[d], rez.at[d], zdev(d))
    for d in NEAR:
        arrive(gwo.at[k * NZ + behind(z, d)], sez.at[d], rez.at[d])
    send(5, gwo.at[pl.ds(k * NZ, NZ)], gwo.at[pl.ds(k * NZ, NZ)], sf, rf, sib)
    for q in range(PARTS):
        for d in NEAR:
            arrive(zr5.at[d, part[q]], s5z.at[q, d], r5z.at[q, d])
            back[q] = back[q] + zr5[d, part[q]].astype(F32)
    gf[...] = (jnp.concatenate(back, axis=0) * nrow).T.astype(BF16)
    stores[1].start()
    arrive(gwo.at[pl.ds((1 - k) * NZ, NZ)], sf, rf)
    for i in range(16):
        rows, cs = slice(i // 2 * 16, i // 2 * 16 + 16), slice(i % 2 * HID // 2, (i % 2 + 1) * HID // 2)
        gw[rows, cs] = gwo[i, :, :HID // 2].astype(F32)
    for c in range(HID // N):
        gb[:, c * N:(c + 1) * N] = gwo[c // 2, :, HID // 2:].astype(F32)[c % 2:c % 2 + 1]
    stores[2].start()
    stores[3].start()
    settle(5)
    for cp in stores:
        cp.wait()


def hand_over(*refs):
    sources, targets, stops, sems = refs[:4], refs[4:8], refs[8:12], refs[12]
    ins = [pltpu.make_async_copy(sources[i], stops[i], sems.at[i]) for i in range(4)]
    outs = [pltpu.make_async_copy(stops[i], targets[i], sems.at[4 + i]) for i in range(4)]
    for cp in ins:
        cp.start()
    for come, go in zip(ins, outs):
        come.wait()
        go.start()
    for cp in outs:
        cp.wait()


def shards(features, degrees, proj_weight, bias, grad_out, tile_slots, tile_values):
    anywhere = pl.BlockSpec(memory_space=pl.ANY)
    sem = pltpu.SemaphoreType.DMA
    tile = lambda *lead: pltpu.VMEM(lead + (N, N), BF16)
    flat = lambda count: pltpu.VMEM((count, N // PARTS, N), BF16)
    wide = lambda kind, *lead: pltpu.VMEM(lead + (WIDE,), kind)
    shapes = (
        jax.ShapeDtypeStruct((N, HID), BF16),
        jax.ShapeDtypeStruct((N, HID), F32),
        jax.ShapeDtypeStruct((1, HID), F32),
        jax.ShapeDtypeStruct((N, N), BF16),
    )
    outs = pl.pallas_call(
        layer,
        name="layer",
        out_shape=shapes,
        in_specs=[anywhere] * 7,
        out_specs=(anywhere,) * 4,
        scratch_shapes=[
            *(pltpu.VMEM(shape.shape, shape.dtype) for shape in shapes),
            pltpu.VMEM((2, K), jnp.int32), pltpu.VMEM((16, N), jnp.int32), pltpu.SMEM((16, N), jnp.int32),
            tile(), pltpu.VMEM((1, N), jnp.int32), pltpu.VMEM((N, HID), BF16), pltpu.VMEM((1, HID), F32),
            pltpu.VMEM((N, HID), BF16),
            tile(K), flat(32), flat(32), pltpu.VMEM((K, N, N), F32),
            tile(8), tile(8), tile(8), tile(8), pltpu.VMEM((N, HID), BF16), flat(16), flat(16),
            tile(2, 8), tile(2, 8), tile(8), tile(8), tile(8), tile(8),
            wide(F32, 2, N), wide(F32, 2, 64), wide(F32, 2, 64), wide(BF16, 8, 16), wide(BF16, 8, 16), wide(BF16, 8, 16),
            wide(F32, 4, 16), wide(BF16, 16, 16),
            sem((12,)), *[sem((PARTS, 8))] * 4, *[sem((PARTS, 2))] * 2, *[sem((PARTS, 8))] * 8,
            *[sem((PARTS, 2))] * 2, *[sem((PARTS, 8))] * 4,
            sem, sem, sem((8,)), sem((8,)), sem((8,)), sem((8,)), sem((3,)), sem((3,)),
            sem((8,)), sem((8,)), sem, sem,
        ],
        compiler_params=pltpu.CompilerParams(
            collective_id=0, has_side_effects=True, vmem_limit_bytes=VMEM_LIMIT),
        cost_estimate=pl.CostEstimate(flops=3 * 10 ** 8, bytes_accessed=2 * 10 ** 6, transcendentals=65536),
    )(tile_slots[0, 0].T, features, degrees.reshape(1, N), proj_weight, bias.reshape(1, HID), grad_out,
      tile_values[0, 0])
    act, gw, gb, gf = pl.pallas_call(
        hand_over,
        name="hand_over",
        out_shape=shapes,
        in_specs=[anywhere] * 4,
        out_specs=(anywhere,) * 4,
        scratch_shapes=[pltpu.VMEM(shape.shape, shape.dtype) for shape in shapes] + [sem((8,))],
        compiler_params=pltpu.CompilerParams(vmem_limit_bytes=VMEM_LIMIT),
    )(*outs)
    return act, gw, gb.reshape(HID), gf


def solution(mesh):
    leaf = P(("row", "col"))
    leaf_rows = P(("row", "col"), None)
    return jax.shard_map(
        shards,
        mesh=mesh,
        in_specs=(leaf_rows, leaf, P(), P(), leaf_rows, P("row", "col", None, None), P("row", "col", None, None, None)),
        out_specs=(leaf_rows, P(), P(), leaf_rows),
        check_vma=False,
    )
```

```python
import jax
import jax.numpy as jnp
from jax import lax
from jax.experimental import pallas as pl
from jax.experimental.pallas import tpu as pltpu
from jax.sharding import PartitionSpec as P

MESH = pl.DeviceIdType.MESH
PARTS = 2
CUTS = (0, 48, 128)
VMEM_LIMIT = 57 * 10 ** 6
BF16 = jnp.bfloat16
F32 = jnp.float32

N = 128
HID = 512
WIDE = HID // 2 + N
K = 32
NZ = 8
FAR = (4, 3, 5, 2, 6, 1, 7)
NEAR = (1, 7, 2, 6, 3, 5, 4)
MIXED = (2, 6, 1, 7, 4, 3, 5)
PERM, COLP, KEEPF, LASTR, HASR, ROWK, KEEPB, LASTC, HASC = range(9)


def index_table(slots):
    rows, cols = slots[0:1, :], slots[1:2, :]
    down = lax.broadcasted_iota(jnp.int32, (K, K), 0)
    along = lax.broadcasted_iota(jnp.int32, (K, K), 1)
    live = rows >= 0
    row_key = jnp.where(live, rows, 16)
    col_key = jnp.where(live, cols, 32)

    def upright(values):
        return jnp.sum(jnp.where(down == along, jnp.broadcast_to(values, (K, K)), 0), axis=1, keepdims=True)

    def place(values, where):
        return jnp.sum(jnp.where(where, jnp.broadcast_to(values, (K, K)), 0), axis=0, keepdims=True)

    def count(where):
        return jnp.sum(where.astype(jnp.int32), axis=0, keepdims=True)

    rows_up, cols_up = upright(row_key), upright(col_key)
    key_up = rows_up * K + down[:, 0:1]
    key = row_key * K + along[0:1, :]
    rank = jnp.sum((jnp.broadcast_to(key, (K, K)) < key_up).astype(jnp.int32), axis=1, keepdims=True)
    here, after = rank == along, rank + 1 == along
    row_here = place(rows_up, here)
    col_here = jnp.minimum(place(cols_up, here), 31)
    spots = (col_here & 1) * 16 + lax.shift_right_logical(col_here, 1)
    return (
        place(down[:, 0:1], here),
        spots,
        (row_here == place(rows_up, after)).astype(jnp.int32),
        jnp.maximum(count(rows_up <= along) - 1, 0),
        (count(rows_up == along) > 0).astype(jnp.int32),
        jnp.minimum(row_key, 15),
        (col_key == place(cols_up, down + 1 == along)).astype(jnp.int32),
        jnp.maximum(count(cols_up <= along) - 1, 0),
        (count(cols_up == along) > 0).astype(jnp.int32),
    )


def layer(slots_hbm, feat_hbm, deg_hbm, w_hbm, bias_hbm, gout_hbm, vals_hbm,
          act_hbm, gw_hbm, gb_hbm, gf_hbm,
          act, gw, gb, gf, slots, tabv, tab, feat, deg, w, bias, gout, vals,
          xg0, xg1, ps, xs2, xr2, ys2, yr2, dpre, bt0, bt1,
          ss5, sr5, xs5, xr5, zs5, zr5,
          gwx, arh_in, arh, zs, zb, yb, xb, gwo,
          load_sem, s1z, r1z, s1x, r1x, s1s, r1s, s2x, r2x, s2y, r2y,
          s4y, r4y, s4x, r4x, s5s, r5s, s5x, r5x, s5z, r5z,
          sa, ra, sbz, rbz, scy, rcy, sdx, rdx, sez, rez, sf, rf):
    row, col = lax.axis_index("row"), lax.axis_index("col")
    x, z, k = row // 16, (row // 2) % NZ, row % 2
    h, y = col // NZ, col % NZ
    xg, bt = (xg0, xg1), (bt0, bt1)
    part = [pl.ds(CUTS[q], CUTS[q + 1] - CUTS[q]) for q in range(PARTS)]

    def leaf(x_, z_, k_):
        return (x_ * NZ + z_) * 2 + k_

    def spot(x_, z_, k_):
        return k_ * 16 + x_ * NZ + z_

    def behind(at, d):
        return (at + NZ - d) % NZ

    def zdev(d):
        return (leaf(x, (z + d) % NZ, k), col)

    def ydev(d):
        return (row, h * NZ + (y + d) % NZ)

    sib = (leaf(x, z, 1 - k), col)
    xl = (leaf(1 - x, z, k), col)
    xh = (row, (1 - h) * NZ + y)
    xlh = (leaf(1 - x, z, k), (1 - h) * NZ + y)

    def copy(src, dst, ssem, rsem, dev):
        return pltpu.make_async_remote_copy(
            src_ref=src, dst_ref=dst, send_sem=ssem, recv_sem=rsem, device_id=dev, device_id_type=MESH)

    sent = {1: [], 2: [], 4: [], 5: []}

    def send(phase, src, dst, ssem, rsem, dev):
        cp = copy(src, dst, ssem, rsem, dev)
        cp.start()
        sent[phase].append(cp)

    def settle(phase):
        for cp in sent[phase]:
            cp.wait_send()

    def arrive(dst, ssem, rsem):
        copy(dst, dst, ssem, rsem, sib).wait_recv()

    barrier = pltpu.get_barrier_semaphore()
    partners = [sib, xl, xh, xlh] + [zdev(d) for d in NEAR] + [ydev(d) for d in NEAR]
    for dev in partners:
        pl.semaphore_signal(barrier, inc=1, device_id=dev, device_id_type=MESH)
    loads = []
    for i, (far, here) in enumerate((
            (deg_hbm, deg), (feat_hbm, feat), (slots_hbm, slots), (vals_hbm, vals), (w_hbm, w), (bias_hbm, bias),
            (gout_hbm, gout))):
        loads.append(pltpu.make_async_copy(far, here, load_sem.at[i]))
        loads[i].start()
    stores = [pltpu.make_async_copy(here, far, load_sem.at[8 + i]) for i, (here, far) in enumerate(
        ((act, act_hbm), (gf, gf_hbm), (gw, gw_hbm), (gb, gb_hbm)))]
    loads[0].wait()
    loads[1].wait()

    nrow = lax.rsqrt(deg[...].astype(F32))
    mine = spot(x, z, k)
    scaled = (feat[...].astype(F32).T * nrow).astype(BF16)
    for q in range(PARTS):
        xg[q][mine] = scaled[CUTS[q]:CUTS[q + 1]]
    pl.semaphore_wait(barrier, len(partners))

    for q in range(PARTS):
        at = xg[q].at[mine]
        for d in MIXED:
            send(1, at, at, s1z.at[q, d], r1z.at[q, d], zdev(d))
        send(1, at, at, s1x.at[q, 0], r1x.at[q, 0], xl)

    loads[2].wait()
    for i, line in enumerate(index_table(slots[...])):
        tabv[i:i + 1, :K] = line
    to_scalar = pltpu.make_async_copy(tabv, tab, load_sem.at[7])
    to_scalar.start()

    def half_to_sib(q, i, x_):
        at = xg[q].at[pl.ds(spot(x_, 0, k), NZ)]
        send(1, at, at, s1s.at[q, i], r1s.at[q, i], sib)

    def half_from_sib(q, i, x_):
        arrive(xg[q].at[pl.ds(spot(x_, 0, 1 - k), NZ)], s1s.at[q, i], r1s.at[q, i])

    for q in range(PARTS):
        for d in NEAR:
            at = xg[q].at[spot(x, behind(z, d), k)]
            arrive(at, s1z.at[q, d], r1z.at[q, d])
            send(1, at, at, s1x.at[q, d], r1x.at[q, d], xl)
        half_to_sib(q, 0, x)
    to_scalar.wait()
    loads[3].wait()

    def row_sum(at, q):
        return ps[tab[LASTR, at], part[q]] * tab[HASR, at].astype(F32)

    for q in range(PARTS):
        for d in (0,) + NEAR:
            arrive(xg[q].at[spot(1 - x, behind(z, d), k)], s1x.at[q, d], r1x.at[q, d])
        half_to_sib(q, 1, 1 - x)
        half_from_sib(q, 0, x)
        half_from_sib(q, 1, 1 - x)

        def forward_turn(turn, total):
            for i in range(8):
                p = turn * 8 + i
                product = lax.dot_general(xg[q][tab[COLP, p]], vals[tab[PERM, p]],
                                          (((1,), (1,)), ((), ())), preferred_element_type=F32)
                total = total * tab[KEEPF, p].astype(F32) + product
                ps[p, part[q]] = total
            return total

        lax.fori_loop(0, K // 8, forward_turn, jnp.zeros((CUTS[q + 1] - CUTS[q], N), F32))
        for d in FAR + (0,):
            xs2[d, part[q]] = row_sum((1 - h) * NZ + (y + d) % NZ, q).astype(BF16)
            send(2, xs2.at[d, part[q]], xr2.at[d, part[q]], s2x.at[q, d], r2x.at[q, d], xh)
    settle(1)
    smooth = [None] * PARTS
    for q in range(PARTS):
        for d in FAR + (0,):
            own = row_sum(h * NZ + (y + d) % NZ, q)
            arrive(xr2.at[d, part[q]], s2x.at[q, d], r2x.at[q, d])
            both = own + xr2[d, part[q]].astype(F32)
            if d:
                ys2[d, part[q]] = both.astype(BF16)
                send(2, ys2.at[d, part[q]], yr2.at[d, part[q]], s2y.at[q, d], r2y.at[q, d], ydev(d))
            else:
                smooth[q] = both
    for i in (4, 5, 6):
        loads[i].wait()
    for q in range(PARTS):
        for d in NEAR:
            arrive(yr2.at[d, part[q]], s2y.at[q, d], r2y.at[q, d])
            smooth[q] = smooth[q] + yr2[d, part[q]].astype(F32)

    smoothed = (jnp.concatenate(smooth, axis=0) * nrow).astype(BF16)
    gwx[...] = jnp.zeros((2, N, WIDE), F32)
    for c in range(HID // N):
        cs = slice(c * N, (c + 1) * N)
        pre = lax.dot_general(smoothed, w[:, cs], (((0,), (0,)), ((), ())), preferred_element_type=F32) + bias[:, cs]
        square = pre * pre
        slope = 0.7978845608028654
        t = jnp.tanh(slope * (pre + 0.044715 * (square * pre)))
        half = 0.5 * (1.0 + t)
        act[:, cs] = (pre * half).astype(BF16)
        slant = half + (0.5 * slope) * pre * (1.0 - t * t) * (1.0 + (3 * 0.044715) * square)
        dp = gout[:, cs].astype(F32) * slant
        gwx[c // 2, c % 2:c % 2 + 1, HID // 2:] = jnp.sum(dp, axis=0, keepdims=True)
        dpre[:, cs] = dp.astype(BF16)
    projected = lax.dot_general(w[...], dpre[...], (((1,), (1,)), ((), ())), preferred_element_type=F32)
    back_in = (projected * nrow).astype(BF16)
    for q in range(PARTS):
        bt[q][col] = back_in[CUTS[q]:CUTS[q + 1]]

    for q in range(PARTS):
        at = bt[q].at[col]
        for d in MIXED:
            send(4, at, at, s4y.at[q, d], r4y.at[q, d], ydev(d))
        send(4, at, at, s4x.at[q, 0], r4x.at[q, 0], xh)
    stores[0].start()
    for i in range(2):
        cs = slice(i * HID // 2, (i + 1) * HID // 2)
        gwx[i, :, :HID // 2] = jnp.dot(smoothed, dpre[:, cs], preferred_element_type=F32)
    ours, theirs = pl.ds(pl.multiple_of(k * 64, 64), 64), pl.ds(pl.multiple_of((1 - k) * 64, 64), 64)
    send(4, gwx.at[:, theirs], arh_in, sa, ra, sib)
    arrive(arh_in, sa, ra)
    arh[...] = gwx[:, ours] + arh_in[...]

    def eighth(at):
        return arh[at % 2, pl.ds(pl.multiple_of(at // 2 * 16, 16), 16)]

    for d in FAR:
        zs[d] = eighth((z + d) % NZ).astype(BF16)
        send(4, zs.at[d], zb.at[d], sbz.at[d], rbz.at[d], zdev(d))
    settle(2)
    for q in range(PARTS):
        for d in NEAR:
            at = bt[q].at[h * NZ + behind(y, d)]
            arrive(at, s4y.at[q, d], r4y.at[q, d])
            send(4, at, at, s4x.at[q, d], r4x.at[q, d], xh)
    chunk = eighth(z)
    for d in NEAR:
        arrive(zb.at[d], sbz.at[d], rbz.at[d])
        chunk = chunk + zb[d].astype(F32)
    yb[y] = chunk.astype(BF16)
    for d in FAR:
        send(4, yb.at[y], yb.at[y], scy.at[d], rcy.at[d], ydev(d))

    def col_sum(at, q):
        return ps[tab[LASTC, at], part[q]] * tab[HASC, at].astype(F32)

    def to_x(q):
        arrive(sr5.at[1, :, part[q]], s5s.at[q, 1], r5s.at[q, 1])
        for d in FAR + (0,):
            xs5[d, part[q]] = (col_sum(leaf(1 - x, (z + d) % NZ, k), q) + sr5[1, d, part[q]].astype(F32)).astype(BF16)
            send(5, xs5.at[d, part[q]], xr5.at[d, part[q]], s5x.at[q, d], r5x.at[q, d], xl)

    for q in range(PARTS):
        for d in (0,) + NEAR:
            arrive(bt[q].at[(1 - h) * NZ + behind(y, d)], s4x.at[q, d], r4x.at[q, d])
        if q:
            to_x(q - 1)

        def back_turn(turn, total):
            for i in range(8):
                p = turn * 8 + i
                product = jnp.dot(bt[q][tab[ROWK, p]], vals[p], preferred_element_type=F32)
                total = total * tab[KEEPB, p].astype(F32) + product
                ps[p, part[q]] = total
            return total

        lax.fori_loop(0, K // 8, back_turn, jnp.zeros((CUTS[q + 1] - CUTS[q], N), F32))
        for a in (1, 0):
            xa = 1 - x if a else x
            for d in range(NZ):
                ss5[a, d, part[q]] = col_sum(leaf(xa, (z + d) % NZ, 1 - k), q).astype(BF16)
            send(5, ss5.at[a, :, part[q]], sr5.at[a, :, part[q]], s5s.at[q, a], r5s.at[q, a], sib)
    for d in NEAR:
        arrive(yb.at[behind(y, d)], scy.at[d], rcy.at[d])
    chunk = yb[0].astype(F32)
    for i in range(1, NZ):
        chunk = chunk + yb[i].astype(F32)
    me = x * 2 + h
    xb[me] = chunk
    send(5, xb.at[me], xb.at[me], sdx.at[0], rdx.at[0], xl)
    send(5, xb.at[me], xb.at[me], sdx.at[1], rdx.at[1], xh)
    send(5, xb.at[me], xb.at[me], sdx.at[2], rdx.at[2], xlh)
    to_x(PARTS - 1)
    settle(4)
    back = [None] * PARTS
    for q in range(PARTS):
        arrive(sr5.at[0, :, part[q]], s5s.at[q, 0], r5s.at[q, 0])
        for d in FAR + (0,):
            own = col_sum(leaf(x, (z + d) % NZ, k), q) + sr5[0, d, part[q]].astype(F32)
            arrive(xr5.at[d, part[q]], s5x.at[q, d], r5x.at[q, d])
            both = own + xr5[d, part[q]].astype(F32)
            if d:
                zs5[d, part[q]] = both.astype(BF16)
                send(5, zs5.at[d, part[q]], zr5.at[d, part[q]], s5z.at[q, d], r5z.at[q, d], zdev(d))
            else:
                back[q] = both
        if q == 0:
            arrive(xb.at[(1 - x) * 2 + h], sdx.at[0], rdx.at[0])
            arrive(xb.at[x * 2 + 1 - h], sdx.at[1], rdx.at[1])
            arrive(xb.at[(1 - x) * 2 + 1 - h], sdx.at[2], rdx.at[2])
            gwo[k * NZ + z] = (((xb[0] + xb[1]) + (xb[2] + xb[3])) * (65536.0 ** -0.5)).astype(BF16)
            for d in FAR:
                send(5, gwo.at[k * NZ + z], gwo.at[k * NZ + z], sez.at[d], rez.at[d], zdev(d))
    for d in NEAR:
        arrive(gwo.at[k * NZ + behind(z, d)], sez.at[d], rez.at[d])
    send(5, gwo.at[pl.ds(k * NZ, NZ)], gwo.at[pl.ds(k * NZ, NZ)], sf, rf, sib)
    for q in range(PARTS):
        for d in NEAR:
            arrive(zr5.at[d, part[q]], s5z.at[q, d], r5z.at[q, d])
            back[q] = back[q] + zr5[d, part[q]].astype(F32)
    gf[...] = (jnp.concatenate(back, axis=0) * nrow).T.astype(BF16)
    stores[1].start()
    arrive(gwo.at[pl.ds((1 - k) * NZ, NZ)], sf, rf)
    for i in range(16):
        rows, cs = slice(i // 2 * 16, i // 2 * 16 + 16), slice(i % 2 * HID // 2, (i % 2 + 1) * HID // 2)
        gw[rows, cs] = gwo[i, :, :HID // 2].astype(F32)
    for c in range(HID // N):
        gb[:, c * N:(c + 1) * N] = gwo[c // 2, :, HID // 2:].astype(F32)[c % 2:c % 2 + 1]
    stores[2].start()
    stores[3].start()
    settle(5)
    for cp in stores:
        cp.wait()


def hand_over(*refs):
    sources, targets, stops, sems = refs[:4], refs[4:8], refs[8:12], refs[12]
    ins = [pltpu.make_async_copy(sources[i], stops[i], sems.at[i]) for i in range(4)]
    outs = [pltpu.make_async_copy(stops[i], targets[i], sems.at[4 + i]) for i in range(4)]
    for cp in ins:
        cp.start()
    for come, go in zip(ins, outs):
        come.wait()
        go.start()
    for cp in outs:
        cp.wait()


def shards(features, degrees, proj_weight, bias, grad_out, tile_slots, tile_values):
    anywhere = pl.BlockSpec(memory_space=pl.ANY)
    sem = pltpu.SemaphoreType.DMA
    tile = lambda *lead: pltpu.VMEM(lead + (N, N), BF16)
    flat = lambda count: [pltpu.VMEM((count, CUTS[q + 1] - CUTS[q], N), BF16) for q in range(PARTS)]
    wide = lambda kind, *lead: pltpu.VMEM(lead + (WIDE,), kind)
    shapes = (
        jax.ShapeDtypeStruct((N, HID), BF16),
        jax.ShapeDtypeStruct((N, HID), F32),
        jax.ShapeDtypeStruct((1, HID), F32),
        jax.ShapeDtypeStruct((N, N), BF16),
    )
    outs = pl.pallas_call(
        layer,
        name="layer",
        out_shape=shapes,
        in_specs=[anywhere] * 7,
        out_specs=(anywhere,) * 4,
        scratch_shapes=[
            *(pltpu.VMEM(shape.shape, shape.dtype) for shape in shapes),
            pltpu.VMEM((2, K), jnp.int32), pltpu.VMEM((16, N), jnp.int32), pltpu.SMEM((16, N), jnp.int32),
            tile(), pltpu.VMEM((1, N), jnp.int32), pltpu.VMEM((N, HID), BF16), pltpu.VMEM((1, HID), F32),
            pltpu.VMEM((N, HID), BF16),
            tile(K), *flat(32), pltpu.VMEM((K, N, N), F32),
            tile(8), tile(8), tile(8), tile(8), pltpu.VMEM((N, HID), BF16), *flat(16),
            tile(2, 8), tile(2, 8), tile(8), tile(8), tile(8), tile(8),
            wide(F32, 2, N), wide(F32, 2, 64), wide(F32, 2, 64), wide(BF16, 8, 16), wide(BF16, 8, 16), wide(BF16, 8, 16),
            wide(F32, 4, 16), wide(BF16, 16, 16),
            sem((12,)), *[sem((PARTS, 8))] * 4, *[sem((PARTS, 2))] * 2, *[sem((PARTS, 8))] * 8,
            *[sem((PARTS, 2))] * 2, *[sem((PARTS, 8))] * 4,
            sem, sem, sem((8,)), sem((8,)), sem((8,)), sem((8,)), sem((3,)), sem((3,)),
            sem((8,)), sem((8,)), sem, sem,
        ],
        compiler_params=pltpu.CompilerParams(
            collective_id=0, has_side_effects=True, vmem_limit_bytes=VMEM_LIMIT),
        cost_estimate=pl.CostEstimate(flops=3 * 10 ** 8, bytes_accessed=2 * 10 ** 6, transcendentals=65536),
    )(tile_slots[0, 0].T, features, degrees.reshape(1, N), proj_weight, bias.reshape(1, HID), grad_out,
      tile_values[0, 0])
    act, gw, gb, gf = pl.pallas_call(
        hand_over,
        name="hand_over",
        out_shape=shapes,
        in_specs=[anywhere] * 4,
        out_specs=(anywhere,) * 4,
        scratch_shapes=[pltpu.VMEM(shape.shape, shape.dtype) for shape in shapes] + [sem((8,))],
        compiler_params=pltpu.CompilerParams(vmem_limit_bytes=VMEM_LIMIT),
    )(*outs)
    return act, gw, gb.reshape(HID), gf


def solution(mesh):
    leaf = P(("row", "col"))
    leaf_rows = P(("row", "col"), None)
    return jax.shard_map(
        shards,
        mesh=mesh,
        in_specs=(leaf_rows, leaf, P(), P(), leaf_rows, P("row", "col", None, None), P("row", "col", None, None, None)),
        out_specs=(leaf_rows, P(), P(), leaf_rows),
        check_vma=False,
    )
```

```python
import jax
import jax.numpy as jnp
from jax import lax
from jax.experimental import pallas as pl
from jax.experimental.pallas import tpu as pltpu
from jax.sharding import PartitionSpec as P

MESH = pl.DeviceIdType.MESH
PARTS = 2
CUTS = (0, 48, 128)
VMEM_LIMIT = 57 * 10 ** 6
BF16 = jnp.bfloat16
F32 = jnp.float32

N = 128
HID = 512
WIDE = HID // 2 + N
K = 32
NZ = 8
FAR = (4, 3, 5, 2, 6, 1, 7)
NEAR = (1, 7, 2, 6, 3, 5, 4)
MIXED = (2, 6, 1, 7, 4, 3, 5)
PERM, COLP, KEEPF, LASTR, HASR, ROWK, KEEPB, LASTC, HASC = range(9)


def index_table(slots):
    rows, cols = slots[0:1, :], slots[1:2, :]
    down = lax.broadcasted_iota(jnp.int32, (K, K), 0)
    along = lax.broadcasted_iota(jnp.int32, (K, K), 1)
    live = rows >= 0
    row_key = jnp.where(live, rows, 16)
    col_key = jnp.where(live, cols, 32)

    def upright(values):
        return jnp.sum(jnp.where(down == along, jnp.broadcast_to(values, (K, K)), 0), axis=1, keepdims=True)

    def place(values, where):
        return jnp.sum(jnp.where(where, jnp.broadcast_to(values, (K, K)), 0), axis=0, keepdims=True)

    def count(where):
        return jnp.sum(where.astype(jnp.int32), axis=0, keepdims=True)

    rows_up, cols_up = upright(row_key), upright(col_key)
    key_up = rows_up * K + down[:, 0:1]
    key = row_key * K + along[0:1, :]
    rank = jnp.sum((jnp.broadcast_to(key, (K, K)) < key_up).astype(jnp.int32), axis=1, keepdims=True)
    here, after = rank == along, rank + 1 == along
    row_here = place(rows_up, here)
    col_here = jnp.minimum(place(cols_up, here), 31)
    spots = (col_here & 1) * 16 + lax.shift_right_logical(col_here, 1)
    return (
        place(down[:, 0:1], here),
        spots,
        (row_here == place(rows_up, after)).astype(jnp.int32),
        jnp.maximum(count(rows_up <= along) - 1, 0),
        (count(rows_up == along) > 0).astype(jnp.int32),
        jnp.minimum(row_key, 15),
        (col_key == place(cols_up, down + 1 == along)).astype(jnp.int32),
        jnp.maximum(count(cols_up <= along) - 1, 0),
        (count(cols_up == along) > 0).astype(jnp.int32),
    )


def layer(slots_hbm, feat_hbm, deg_hbm, w_hbm, bias_hbm, gout_hbm, vals_hbm,
          act_hbm, gw_hbm, gb_hbm, gf_hbm,
          act, gw, gb, gf, slots, tabv, tab, feat, deg, w, bias, gout, vals,
          xg0, xg1, ps, xs2, xr2, ys2, yr2, dpre, bt0, bt1,
          ss5, sr5, xs5, xr5, zs5, zr5,
          gwx, arh_in, arh, zs, zb, yb, xb, gwo,
          load_sem, s1z, r1z, s1x, r1x, s1s, r1s, s2x, r2x, s2y, r2y,
          s4y, r4y, s4x, r4x, s5s, r5s, s5x, r5x, s5z, r5z,
          sa, ra, sbz, rbz, scy, rcy, sdx, rdx, sez, rez, sf, rf):
    row, col = lax.axis_index("row"), lax.axis_index("col")
    x, z, k = row // 16, (row // 2) % NZ, row % 2
    h, y = col // NZ, col % NZ
    xg, bt = (xg0, xg1), (bt0, bt1)
    part = [pl.ds(CUTS[q], CUTS[q + 1] - CUTS[q]) for q in range(PARTS)]

    def leaf(x_, z_, k_):
        return (x_ * NZ + z_) * 2 + k_

    def spot(x_, z_, k_):
        return k_ * 16 + x_ * NZ + z_

    def behind(at, d):
        return (at + NZ - d) % NZ

    def zdev(d):
        return (leaf(x, (z + d) % NZ, k), col)

    def ydev(d):
        return (row, h * NZ + (y + d) % NZ)

    sib = (leaf(x, z, 1 - k), col)
    xl = (leaf(1 - x, z, k), col)
    xh = (row, (1 - h) * NZ + y)
    xlh = (leaf(1 - x, z, k), (1 - h) * NZ + y)

    def copy(src, dst, ssem, rsem, dev):
        return pltpu.make_async_remote_copy(
            src_ref=src, dst_ref=dst, send_sem=ssem, recv_sem=rsem, device_id=dev, device_id_type=MESH)

    sent = {1: [], 2: [], 4: [], 5: []}

    def send(phase, src, dst, ssem, rsem, dev):
        cp = copy(src, dst, ssem, rsem, dev)
        cp.start()
        sent[phase].append(cp)

    def settle(phase):
        for cp in sent[phase]:
            cp.wait_send()

    def arrive(dst, ssem, rsem):
        copy(dst, dst, ssem, rsem, sib).wait_recv()

    barrier = pltpu.get_barrier_semaphore()
    partners = [sib, xl, xh, xlh] + [zdev(d) for d in NEAR] + [ydev(d) for d in NEAR]
    for dev in partners:
        pl.semaphore_signal(barrier, inc=1, device_id=dev, device_id_type=MESH)
    loads = []
    for i, (far, here) in enumerate((
            (deg_hbm, deg), (feat_hbm, feat), (slots_hbm, slots), (vals_hbm, vals), (w_hbm, w), (bias_hbm, bias),
            (gout_hbm, gout))):
        loads.append(pltpu.make_async_copy(far, here, load_sem.at[i]))
        loads[i].start()
    stores = [pltpu.make_async_copy(here, far, load_sem.at[8 + i]) for i, (here, far) in enumerate(
        ((act, act_hbm), (gf, gf_hbm), (gw, gw_hbm), (gb, gb_hbm)))]
    loads[0].wait()
    loads[1].wait()

    nrow = lax.rsqrt(deg[...].astype(F32))
    mine = spot(x, z, k)
    scaled = (feat[...].astype(F32).T * nrow).astype(BF16)
    for q in range(PARTS):
        xg[q][mine] = scaled[CUTS[q]:CUTS[q + 1]]
    pl.semaphore_wait(barrier, len(partners))

    for q in range(PARTS):
        at = xg[q].at[mine]
        for d in MIXED:
            send(1, at, at, s1z.at[q, d], r1z.at[q, d], zdev(d))
        send(1, at, at, s1x.at[q, 0], r1x.at[q, 0], xl)

    loads[2].wait()
    for i, line in enumerate(index_table(slots[...])):
        tabv[i:i + 1, :K] = line
    to_scalar = pltpu.make_async_copy(tabv, tab, load_sem.at[7])
    to_scalar.start()

    def half_to_sib(q, i, x_):
        at = xg[q].at[pl.ds(spot(x_, 0, k), NZ)]
        send(1, at, at, s1s.at[q, i], r1s.at[q, i], sib)

    def half_from_sib(q, i, x_):
        arrive(xg[q].at[pl.ds(spot(x_, 0, 1 - k), NZ)], s1s.at[q, i], r1s.at[q, i])

    for q in range(PARTS):
        for d in NEAR:
            at = xg[q].at[spot(x, behind(z, d), k)]
            arrive(at, s1z.at[q, d], r1z.at[q, d])
            send(1, at, at, s1x.at[q, d], r1x.at[q, d], xl)
        half_to_sib(q, 0, x)
    to_scalar.wait()
    loads[3].wait()

    def row_sum(at, q):
        return ps[tab[LASTR, at], part[q]] * tab[HASR, at].astype(F32)

    for q in range(PARTS):
        for d in (0,) + NEAR:
            arrive(xg[q].at[spot(1 - x, behind(z, d), k)], s1x.at[q, d], r1x.at[q, d])
        half_to_sib(q, 1, 1 - x)
        half_from_sib(q, 0, x)
        half_from_sib(q, 1, 1 - x)

        def forward_turn(turn, total):
            for i in range(8):
                p = turn * 8 + i
                product = lax.dot_general(xg[q][tab[COLP, p]], vals[tab[PERM, p]],
                                          (((1,), (1,)), ((), ())), preferred_element_type=F32)
                total = total * tab[KEEPF, p].astype(F32) + product
                ps[p, part[q]] = total
            return total

        lax.fori_loop(0, K // 8, forward_turn, jnp.zeros((CUTS[q + 1] - CUTS[q], N), F32))
        for d in FAR + (0,):
            xs2[d, part[q]] = row_sum((1 - h) * NZ + (y + d) % NZ, q).astype(BF16)
            send(2, xs2.at[d, part[q]], xr2.at[d, part[q]], s2x.at[q, d], r2x.at[q, d], xh)
    settle(1)
    smooth = [None] * PARTS
    for q in range(PARTS):
        for d in FAR + (0,):
            own = row_sum(h * NZ + (y + d) % NZ, q)
            arrive(xr2.at[d, part[q]], s2x.at[q, d], r2x.at[q, d])
            both = own + xr2[d, part[q]].astype(F32)
            if d:
                ys2[d, part[q]] = both.astype(BF16)
                send(2, ys2.at[d, part[q]], yr2.at[d, part[q]], s2y.at[q, d], r2y.at[q, d], ydev(d))
            else:
                smooth[q] = both
    for i in (4, 5, 6):
        loads[i].wait()
    for q in range(PARTS):
        for d in NEAR:
            arrive(yr2.at[d, part[q]], s2y.at[q, d], r2y.at[q, d])
            smooth[q] = smooth[q] + yr2[d, part[q]].astype(F32)

    smoothed = (jnp.concatenate(smooth, axis=0) * nrow).astype(BF16)
    gwx[...] = jnp.zeros((2, N, WIDE), F32)
    for c in range(HID // N):
        cs = slice(c * N, (c + 1) * N)
        pre = lax.dot_general(smoothed, w[:, cs], (((0,), (0,)), ((), ())), preferred_element_type=F32) + bias[:, cs]
        square = pre * pre
        slope = 0.7978845608028654
        t = jnp.tanh(slope * (pre + 0.044715 * (square * pre)))
        half = 0.5 * (1.0 + t)
        act[:, cs] = (pre * half).astype(BF16)
        slant = half + (0.5 * slope) * pre * (1.0 - t * t) * (1.0 + (3 * 0.044715) * square)
        dp = gout[:, cs].astype(F32) * slant
        gwx[c // 2, c % 2:c % 2 + 1, HID // 2:] = jnp.sum(dp, axis=0, keepdims=True)
        dpre[:, cs] = dp.astype(BF16)
    projected = lax.dot_general(w[...], dpre[...], (((1,), (1,)), ((), ())), preferred_element_type=F32)
    back_in = (projected * nrow).astype(BF16)
    for q in range(PARTS):
        bt[q][col] = back_in[CUTS[q]:CUTS[q + 1]]

    for q in range(PARTS):
        at = bt[q].at[col]
        for d in MIXED:
            send(4, at, at, s4y.at[q, d], r4y.at[q, d], ydev(d))
        send(4, at, at, s4x.at[q, 0], r4x.at[q, 0], xh)
    stores[0].start()
    for i in range(2):
        cs = slice(i * HID // 2, (i + 1) * HID // 2)
        gwx[i, :, :HID // 2] = jnp.dot(smoothed, dpre[:, cs], preferred_element_type=F32)
    ours, theirs = pl.ds(pl.multiple_of(k * 64, 64), 64), pl.ds(pl.multiple_of((1 - k) * 64, 64), 64)
    send(4, gwx.at[:, theirs], arh_in, sa, ra, sib)
    arrive(arh_in, sa, ra)
    arh[...] = gwx[:, ours] + arh_in[...]

    def eighth(at):
        return arh[at % 2, pl.ds(pl.multiple_of(at // 2 * 16, 16), 16)]

    for d in FAR:
        zs[d] = eighth((z + d) % NZ).astype(BF16)
        send(4, zs.at[d], zb.at[d], sbz.at[d], rbz.at[d], zdev(d))
    settle(2)
    for q in range(PARTS):
        for d in NEAR:
            at = bt[q].at[h * NZ + behind(y, d)]
            arrive(at, s4y.at[q, d], r4y.at[q, d])
            send(4, at, at, s4x.at[q, d], r4x.at[q, d], xh)
    chunk = eighth(z)
    for d in NEAR:
        arrive(zb.at[d], sbz.at[d], rbz.at[d])
        chunk = chunk + zb[d].astype(F32)
    yb[y] = chunk.astype(BF16)
    for d in FAR:
        send(4, yb.at[y], yb.at[y], scy.at[d], rcy.at[d], ydev(d))

    def col_sum(at, q):
        return ps[tab[LASTC, at], part[q]] * tab[HASC, at].astype(F32)

    def to_x(q):
        arrive(sr5.at[1, :, part[q]], s5s.at[q, 1], r5s.at[q, 1])
        for d in FAR + (0,):
            xs5[d, part[q]] = (col_sum(leaf(1 - x, (z + d) % NZ, k), q) + sr5[1, d, part[q]].astype(F32)).astype(BF16)
            send(5, xs5.at[d, part[q]], xr5.at[d, part[q]], s5x.at[q, d], r5x.at[q, d], xl)

    for q in range(PARTS):
        for d in (0,) + NEAR:
            arrive(bt[q].at[(1 - h) * NZ + behind(y, d)], s4x.at[q, d], r4x.at[q, d])
        if q:
            to_x(q - 1)

        def back_turn(turn, total):
            for i in range(8):
                p = turn * 8 + i
                product = jnp.dot(bt[q][tab[ROWK, p]], vals[p], preferred_element_type=F32)
                total = total * tab[KEEPB, p].astype(F32) + product
                ps[p, part[q]] = total
            return total

        lax.fori_loop(0, K // 8, back_turn, jnp.zeros((CUTS[q + 1] - CUTS[q], N), F32))
        for a in (1, 0):
            xa = 1 - x if a else x
            for d in range(NZ):
                ss5[a, d, part[q]] = col_sum(leaf(xa, (z + d) % NZ, 1 - k), q).astype(BF16)
            send(5, ss5.at[a, :, part[q]], sr5.at[a, :, part[q]], s5s.at[q, a], r5s.at[q, a], sib)
    for d in NEAR:
        arrive(yb.at[behind(y, d)], scy.at[d], rcy.at[d])
    chunk = yb[0].astype(F32)
    for i in range(1, NZ):
        chunk = chunk + yb[i].astype(F32)
    me = x * 2 + h
    xb[me] = chunk
    send(5, xb.at[me], xb.at[me], sdx.at[0], rdx.at[0], xl)
    send(5, xb.at[me], xb.at[me], sdx.at[1], rdx.at[1], xh)
    send(5, xb.at[me], xb.at[me], sdx.at[2], rdx.at[2], xlh)
    to_x(PARTS - 1)
    settle(4)
    back = [None] * PARTS
    for q in range(PARTS):
        arrive(sr5.at[0, :, part[q]], s5s.at[q, 0], r5s.at[q, 0])
        for d in FAR + (0,):
            own = col_sum(leaf(x, (z + d) % NZ, k), q) + sr5[0, d, part[q]].astype(F32)
            arrive(xr5.at[d, part[q]], s5x.at[q, d], r5x.at[q, d])
            both = own + xr5[d, part[q]].astype(F32)
            if d:
                zs5[d, part[q]] = both.astype(BF16)
                send(5, zs5.at[d, part[q]], zr5.at[d, part[q]], s5z.at[q, d], r5z.at[q, d], zdev(d))
            else:
                back[q] = both
        if q == 0:
            arrive(xb.at[(1 - x) * 2 + h], sdx.at[0], rdx.at[0])
            arrive(xb.at[x * 2 + 1 - h], sdx.at[1], rdx.at[1])
            arrive(xb.at[(1 - x) * 2 + 1 - h], sdx.at[2], rdx.at[2])
            gwo[k * NZ + z] = (((xb[0] + xb[1]) + (xb[2] + xb[3])) * (65536.0 ** -0.5)).astype(BF16)
            for d in FAR:
                send(5, gwo.at[k * NZ + z], gwo.at[k * NZ + z], sez.at[d], rez.at[d], zdev(d))
    for d in NEAR:
        arrive(gwo.at[k * NZ + behind(z, d)], sez.at[d], rez.at[d])
    send(5, gwo.at[pl.ds(k * NZ, NZ)], gwo.at[pl.ds(k * NZ, NZ)], sf, rf, sib)
    for q in range(PARTS):
        for d in NEAR:
            arrive(zr5.at[d, part[q]], s5z.at[q, d], r5z.at[q, d])
            back[q] = back[q] + zr5[d, part[q]].astype(F32)
    gf[...] = (jnp.concatenate(back, axis=0) * nrow).T.astype(BF16)
    stores[1].start()

    def unpack(k_):
        for i in range(8):
            rows = pl.ds(pl.multiple_of(k_ * 64 + i // 2 * 16, 16), 16)
            gw[rows, i % 2 * HID // 2:(i % 2 + 1) * HID // 2] = gwo[k_ * NZ + i, :, :HID // 2].astype(F32)

    unpack(k)
    arrive(gwo.at[pl.ds((1 - k) * NZ, NZ)], sf, rf)
    unpack(1 - k)
    for c in range(HID // N):
        gb[:, c * N:(c + 1) * N] = gwo[c // 2, :, HID // 2:].astype(F32)[c % 2:c % 2 + 1]
    stores[2].start()
    stores[3].start()
    settle(5)
    for cp in stores:
        cp.wait()


def hand_over(*refs):
    sources, targets, stops, sems = refs[:4], refs[4:8], refs[8:12], refs[12]
    ins = [pltpu.make_async_copy(sources[i], stops[i], sems.at[i]) for i in range(4)]
    outs = [pltpu.make_async_copy(stops[i], targets[i], sems.at[4 + i]) for i in range(4)]
    for cp in ins:
        cp.start()
    for come, go in zip(ins, outs):
        come.wait()
        go.start()
    for cp in outs:
        cp.wait()


def shards(features, degrees, proj_weight, bias, grad_out, tile_slots, tile_values):
    anywhere = pl.BlockSpec(memory_space=pl.ANY)
    sem = pltpu.SemaphoreType.DMA
    tile = lambda *lead: pltpu.VMEM(lead + (N, N), BF16)
    flat = lambda count: [pltpu.VMEM((count, CUTS[q + 1] - CUTS[q], N), BF16) for q in range(PARTS)]
    wide = lambda kind, *lead: pltpu.VMEM(lead + (WIDE,), kind)
    shapes = (
        jax.ShapeDtypeStruct((N, HID), BF16),
        jax.ShapeDtypeStruct((N, HID), F32),
        jax.ShapeDtypeStruct((1, HID), F32),
        jax.ShapeDtypeStruct((N, N), BF16),
    )
    outs = pl.pallas_call(
        layer,
        name="layer",
        out_shape=shapes,
        in_specs=[anywhere] * 7,
        out_specs=(anywhere,) * 4,
        scratch_shapes=[
            *(pltpu.VMEM(shape.shape, shape.dtype) for shape in shapes),
            pltpu.VMEM((2, K), jnp.int32), pltpu.VMEM((16, N), jnp.int32), pltpu.SMEM((16, N), jnp.int32),
            tile(), pltpu.VMEM((1, N), jnp.int32), pltpu.VMEM((N, HID), BF16), pltpu.VMEM((1, HID), F32),
            pltpu.VMEM((N, HID), BF16),
            tile(K), *flat(32), pltpu.VMEM((K, N, N), F32),
            tile(8), tile(8), tile(8), tile(8), pltpu.VMEM((N, HID), BF16), *flat(16),
            tile(2, 8), tile(2, 8), tile(8), tile(8), tile(8), tile(8),
            wide(F32, 2, N), wide(F32, 2, 64), wide(F32, 2, 64), wide(BF16, 8, 16), wide(BF16, 8, 16), wide(BF16, 8, 16),
            wide(F32, 4, 16), wide(BF16, 16, 16),
            sem((12,)), *[sem((PARTS, 8))] * 4, *[sem((PARTS, 2))] * 2, *[sem((PARTS, 8))] * 8,
            *[sem((PARTS, 2))] * 2, *[sem((PARTS, 8))] * 4,
            sem, sem, sem((8,)), sem((8,)), sem((8,)), sem((8,)), sem((3,)), sem((3,)),
            sem((8,)), sem((8,)), sem, sem,
        ],
        compiler_params=pltpu.CompilerParams(
            collective_id=0, has_side_effects=True, vmem_limit_bytes=VMEM_LIMIT),
        cost_estimate=pl.CostEstimate(flops=3 * 10 ** 8, bytes_accessed=2 * 10 ** 6, transcendentals=65536),
    )(tile_slots[0, 0].T, features, degrees.reshape(1, N), proj_weight, bias.reshape(1, HID), grad_out,
      tile_values[0, 0])
    act, gw, gb, gf = pl.pallas_call(
        hand_over,
        name="hand_over",
        out_shape=shapes,
        in_specs=[anywhere] * 4,
        out_specs=(anywhere,) * 4,
        scratch_shapes=[pltpu.VMEM(shape.shape, shape.dtype) for shape in shapes] + [sem((8,))],
        compiler_params=pltpu.CompilerParams(vmem_limit_bytes=VMEM_LIMIT),
    )(*outs)
    return act, gw, gb.reshape(HID), gf


def solution(mesh):
    leaf = P(("row", "col"))
    leaf_rows = P(("row", "col"), None)
    return jax.shard_map(
        shards,
        mesh=mesh,
        in_specs=(leaf_rows, leaf, P(), P(), leaf_rows, P("row", "col", None, None), P("row", "col", None, None, None)),
        out_specs=(leaf_rows, P(), P(), leaf_rows),
        check_vma=False,
    )
```
